256 devices in a mesh: seq: 4 (over y), res: 64 (over x, z, core).
Axes of the slice: x: 4, y: 4, z: 8, core: 2. Of those that a mesh axis runs over, the one named last changes fastest.
Arguments:
- alignment: int32 [3072, 1024], P(None, 'seq'), may hold values from 0 to 20
- seq_weights: float32 [1024], P('seq'), may hold values from 0.1 to 1
- fields: float32 [3072, 21], P('res'), may hold values from -4 to 352
- couplings: bfloat16 [32768, 441], P('res'), may hold values from -2.390625 to 2.390625
- pair_left: int32 [32768], P('res'), may hold values from 0 to 47, as said below
- pair_slot: int32 [32768], P('res'), may hold values from 0 to 3
- slot_residue: int32 [16384], P('res'), may hold values from 0 to 47
- pair_count: int32 [4096], P('res'), may hold values from 1 to 8, as said below
Outputs:
- coupling_grad: float32 [32768, 441], P('res')
- field_grad: float32 [3072, 21], P('res')
The draws below stay inside these ranges and needn't reach their ends.
Inputs may be any that keep to these rules, and one draw needn't show every extreme that they name: `pair_left`: A residue never pairs with itself; the same two residues may form more than one pair. Only the first pair_count slots of each bucket are live.
All inputs are finite; a program needn't handle non-finite values.
Results may differ from the reference program's by a relative error of at most 0.003.
Values may be sent and summed in bfloat16 or wider, within the bound.
No kernel may reach another device: no remote copies, remote signals or barrier semaphores. Data moves between devices by JAX's collectives and lax.ppermute only.
A program may use at most 128 MiB of HBM per device.

```python
import math
import jax
import jax.numpy as jnp
from jax import lax

Q = 21
QQ = 441
RES_DEV = 48
CAP = 8
SLOTS = 4
RES = 3072
SEQS = 1024
PAIR_DEV = 512
PAIRS = 32768
N_RES = 64


def pair_plan(key):
    subkeys = jax.random.split(key, 3)
    slots_drawn = jax.random.randint(subkeys[0], (N_RES * N_RES * SLOTS,), 0, RES_DEV)
    slot_pick = jax.random.randint(subkeys[1], (PAIRS,), 0, SLOTS)
    left_pick = jax.random.randint(subkeys[2], (PAIRS,), 0, RES_DEV)
    pair_index = jnp.arange(PAIRS, dtype=jnp.int32)
    owner_dev = pair_index // PAIR_DEV
    target = pair_index % PAIR_DEV // CAP
    partner = slots_drawn[(owner_dev * N_RES + target) * SLOTS + slot_pick]
    clash = (owner_dev == target) & (left_pick == partner)
    left_pick = jnp.where(clash, (left_pick + 1) % RES_DEV, left_pick)
    return (slots_drawn, slot_pick, left_pick)


def draw_slot_residue(key, part):
    return pair_plan(key)[0].astype(jnp.int32)


def draw_pair_slot(key, part):
    return pair_plan(key)[1].astype(jnp.int32)


def draw_pair_left(key, part):
    return pair_plan(key)[2].astype(jnp.int32)


def draw_pair_count(key, part):
    key = jax.random.fold_in(key, 7)
    subkeys = jax.random.split(key, 3)
    devices = jnp.arange(N_RES, dtype=jnp.int32)
    hot_device = jax.random.randint(subkeys[0], (), 0, N_RES)
    load_level = jax.random.randint(subkeys[1], (N_RES,), 1, 5)
    load_level = jnp.where(devices == hot_device, 4, load_level)
    base_count = jax.random.randint(subkeys[2], (N_RES, N_RES), CAP // 2, CAP + 1)
    live_count = jnp.maximum(1, base_count * load_level[:, None] // 4)
    corner = (devices[:, None] == hot_device) & (devices[None, :] == 0)
    live_count = jnp.where(corner, CAP, live_count)
    return live_count.reshape(N_RES * N_RES).astype(jnp.int32)


def draw_fields(key, part):
    key = jax.random.fold_in(key, 11)
    subkeys = jax.random.split(key, 1)
    return jnp.clip(jax.random.normal(subkeys[0], (RES, Q), jnp.float32), -4.0, 4.0)


def set_ends(values, rng, low, high):
    index_at = [jax.random.randint(jax.random.fold_in(rng, axis), (), 0, length) for axis, length in enumerate(values.shape)]
    longest = values.shape.index(max(values.shape))
    next_to = index_at[:longest] + [(index_at[longest] + 1) % values.shape[longest]] + index_at[longest + 1:]
    return values.at[tuple(index_at)].set(low).at[tuple(next_to)].set(high)


def levels(rng, extent, shards, smallest, top_value):
    level, own = 1.0, jax.random.fold_in(rng, 6)
    for axis_at, parts in shards:
        steps = jnp.exp(jax.random.uniform(jax.random.fold_in(own, axis_at), (parts,), jnp.float32, smallest / len(shards), top_value / len(shards)))
        level = level * jnp.repeat(steps, extent[axis_at] // parts).reshape([-1 if axis == axis_at else 1 for axis in range(len(extent))])
    return level


def centred(rng, dims, spread, limit, shards=(), kind=jnp.bfloat16):
    result = spread * jax.random.normal(rng, dims, jnp.float32)
    if shards:
        result = result * levels(rng, dims, shards, -0.22, 0.18)
    return jnp.clip(result, -limit, limit).astype(kind)


def setup_inputs(seed: int = 0) -> dict:
    streams_of = jax.random.split(jax.random.key(seed), 9)
    return {
        "alignment": set_ends(jax.random.randint(streams_of[0], (RES, SEQS), 0, Q), jax.random.fold_in(streams_of[0], 1), 0, Q - 1).astype(jnp.int32),
        "seq_weights": jnp.clip(jnp.exp(math.log(1.0) - 2.3025851 * jax.random.uniform(streams_of[1], (SEQS,), jnp.float32) ** levels(streams_of[1], (SEQS,), ((0, 4),), -0.2, 0.2)), 0.1, 1.0),
        "fields": draw_fields(jax.random.fold_in(streams_of[8], 71), 0),
        "couplings": centred(streams_of[3], (PAIRS, QQ), 0.4, 2.390625, ((0, 64),)),
        "pair_left": draw_pair_left(jax.random.fold_in(streams_of[8], 71), 0),
        "pair_slot": draw_pair_slot(jax.random.fold_in(streams_of[8], 71), 0),
        "slot_residue": draw_slot_residue(jax.random.fold_in(streams_of[8], 71), 0),
        "pair_count": draw_pair_count(jax.random.fold_in(streams_of[8], 71), 0),
    }


def pick_columns(matrix, states):
    return matrix[:, states]


def pick_rows(matrix, states):
    return matrix[states, :].T


def sum_left(resid, states):
    return jax.ops.segment_sum(resid.T, states, num_segments=Q).T


def sum_right(resid, states):
    return jax.ops.segment_sum(resid.T, states, num_segments=Q)


def reference(alignment, seq_weights, fields, couplings, pair_left, pair_slot, slot_residue, pair_count):
    pair_index = jnp.arange(PAIRS, dtype=jnp.int32)
    owner_dev = pair_index // PAIR_DEV
    target_dev = (pair_index % PAIR_DEV) // CAP
    bucket = owner_dev * N_RES + target_dev
    is_live = (pair_index % CAP) < pair_count[bucket]
    left_res = (owner_dev * RES_DEV + pair_left).astype(jnp.int32)
    right_res = (target_dev * RES_DEV + slot_residue[bucket * SLOTS + pair_slot]).astype(jnp.int32)
    live_float = is_live.astype(jnp.float32)
    matrices = couplings.astype(jnp.float32).reshape(PAIRS, Q, Q) * live_float[:, None, None]
    block_rows = math.gcd(PAIRS, 512)
    block_count = PAIRS // block_rows

    def blockwise(array):
        return array.reshape((block_count, block_rows) + array.shape[1:])

    def add_terms(field_sum, inputs):
        matrix, left_part, right_part = inputs
        left_states = alignment[left_part]
        right_states = alignment[right_part]
        near_term = jax.vmap(pick_columns)(matrix, right_states)
        far_term = jax.vmap(pick_rows)(matrix, left_states)
        field_sum = field_sum.at[left_part].add(near_term).at[right_part].add(far_term)
        return field_sum, None

    start_field = jnp.zeros((RES, Q, SEQS), jnp.float32)
    field_sum, unused = lax.scan(add_terms, start_field, (blockwise(matrices), blockwise(left_res), blockwise(right_res)))
    logits = field_sum + fields[:, :, None]
    softmax_out = jax.nn.softmax(logits, axis=1)
    state_codes = jnp.arange(Q, dtype=jnp.int32)
    state_hot = (alignment[:, None, :] == state_codes[None, :, None]).astype(jnp.float32)
    residual = (seq_weights[None, None, :] * (softmax_out - state_hot)).astype(jnp.bfloat16)
    scale = Q / SEQS
    field_grad = scale * jnp.sum(residual.astype(jnp.float32), axis=2)

    def block_grads(inputs):
        left_part, right_part = inputs
        left_states = alignment[left_part]
        right_states = alignment[right_part]
        left_resid = residual[left_part].astype(jnp.float32)
        right_resid = residual[right_part].astype(jnp.float32)
        left_grad = jax.vmap(sum_left)(left_resid, right_states)
        right_grad = jax.vmap(sum_right)(right_resid, left_states)
        return left_grad + right_grad

    gradient = lax.map(block_grads, (blockwise(left_res), blockwise(right_res))).reshape(PAIRS, Q, Q)
    coupling_grad = (gradient * (scale * live_float)[:, None, None]).reshape(PAIRS, Q * Q)
    return coupling_grad, field_grad
```

```python
import functools

import jax
import jax.numpy as jnp
from jax import lax
from jax.experimental import pallas as pl
from jax.experimental.pallas import tpu as pltpu
from jax.sharding import PartitionSpec as P

Q = 21
QP = 24
RL = 48
CAP = 8
SLOTS = 4
PAIRS = 512
BLOCKS = 64
SEQ = 256
RES = 3072
TILE = 128
TILES = PAIRS // TILE
GROUP = 8
GROUPS = RL // GROUP
GROWS = GROUP * QP
QUARTER = 112
PADQ = 4 * QUARTER
DEEP = Q * TILE
F32 = jnp.float32
BF16 = jnp.bfloat16
VMEM = pl.BlockSpec(memory_space=pltpu.VMEM)
SMEM = pl.BlockSpec(memory_space=pltpu.SMEM)
PARAMS = pltpu.CompilerParams(vmem_limit_bytes=56 * 1024 * 1024)


def iota(shape, dim):
    return lax.broadcasted_iota(jnp.int32, shape, dim)


def dot(x, y):
    return jnp.dot(x, y, preferred_element_type=F32)


def pack_kernel(ids, coup, left, slot, table, out, wide, tall):
    wide[...] = jnp.zeros_like(wide)
    wide[0 : Q * Q, :] = coup[...].astype(F32)
    start = pl.multiple_of(ids[0] * QUARTER, 8)
    tall[0:QUARTER, :] = wide[pl.ds(start, QUARTER), :]
    bucket = iota((BLOCKS, PAIRS), 1) // CAP
    spread = (bucket == iota((BLOCKS, PAIRS), 0)).astype(F32).astype(BF16)
    rows = dot(table[...], spread)
    slots = slot[...]
    partner = jnp.zeros((1, PAIRS), F32)
    for s in range(SLOTS):
        partner = partner + jnp.where(slots == s, rows[s : s + 1], 0.0)
    lane = iota((1, PAIRS), 1)
    live = jnp.where((lane % CAP).astype(F32) < rows[SLOTS : SLOTS + 1], 1.0, 0.0)
    sub = iota((16, PAIRS), 0)
    index = jnp.where(sub == 0, left[...].astype(F32), 0.0)
    index = jnp.where(sub == 1, partner, index)
    index = jnp.where(sub == 2, live, index)
    index = jnp.where(sub == 3, ids[1].astype(F32), index)
    index = jnp.where(sub == 4, (lane // CAP).astype(F32), index)
    tall[QUARTER:TILE, :] = index
    out[...] = jnp.transpose(tall[...]).astype(BF16)


def pack_pairs(ids, coup, left, slot, table):
    return pl.pallas_call(
        pack_kernel,
        out_shape=jax.ShapeDtypeStruct((PAIRS, TILE), BF16),
        in_specs=[SMEM, VMEM, VMEM, VMEM, VMEM],
        out_specs=VMEM,
        scratch_shapes=[pltpu.VMEM((PADQ, PAIRS), F32), pltpu.VMEM((TILE, PAIRS), F32)],
        compiler_params=PARAMS,
        name="pack_pairs",
    )(ids, coup, left, slot, table)


def order_half(pack, flipped, own):
    mine, other, block = (112, 113, 116) if own else (113, 112, 115)
    wide = pack.astype(F32)
    key_row = jnp.where(flipped[114:115] > 0.5, flipped[mine : mine + 1], float(RL))
    key_col = jnp.where(wide[:, 114:115] > 0.5, wide[:, mine : mine + 1], float(RL))
    lane = iota((PAIRS, PAIRS), 1).astype(F32)
    sub = iota((PAIRS, PAIRS), 0).astype(F32)
    full_row = key_row * PAIRS + lane
    full_col = key_col * PAIRS + sub
    place_row = jnp.sum(jnp.where(full_col < full_row, 1.0, 0.0), axis=0, keepdims=True)
    place_col = jnp.sum(jnp.where(full_row < full_col, 1.0, 0.0), axis=1, keepdims=True)
    to_sorted = jnp.where(place_col == lane, 1.0, 0.0).astype(BF16)
    to_plain = jnp.where(place_row == sub, 1.0, 0.0).astype(BF16)
    cols = dot(to_plain, pack)
    far = cols[:, block : block + 1] * RL + cols[:, other : other + 1]
    keys = dot(jnp.broadcast_to(key_row, (8, PAIRS)).astype(BF16), to_sorted)
    return to_sorted, to_plain, far, keys


def fill_hot(far, states, hot):
    far_states = jnp.zeros((PAIRS, SEQ), F32)
    chunk = 256
    lane = iota((PAIRS, chunk), 1).astype(F32)
    for n in range(RES // chunk):
        pick = jnp.where(far - float(n * chunk) == lane, 1.0, 0.0).astype(BF16)
        far_states = far_states + dot(pick, states[n * chunk : (n + 1) * chunk, :])
    for c in range(Q):
        hit = jnp.where(far_states == float(c), 1.0, 0.0).astype(BF16)
        for j in range(TILES):
            hot[j, c * TILE : (c + 1) * TILE, :] = hit[j * TILE : (j + 1) * TILE]


def store_keys(keys, keys_ref):
    for j in range(TILES):
        keys_ref[j] = keys[:, j * TILE : (j + 1) * TILE]


def group_range(keys):
    low = jnp.min(keys).astype(jnp.int32)
    high = jnp.max(jnp.where(keys < RL - 0.5, keys, -1.0)).astype(jnp.int32)
    return lax.shift_right_logical(low, 3), lax.shift_right_logical(high + 8, 3)


def group_masks(keys, g):
    base = (g * GROUP).astype(F32)
    wide = jnp.broadcast_to(keys[0:1], (QP, TILE))
    return [wide == base + float(m) for m in range(GROUP)]


def add_field(keys_ref, blocks, hot, lhs, field):
    def tile_step(j, carry):
        keys = keys_ref[j]
        low, high = group_range(keys)

        def group_step(g, carry):
            masks = group_masks(keys, g)
            for c in range(Q):
                block = blocks[j, c]
                rows = [jnp.where(mask, block, 0.0) for mask in masks]
                lhs[:, c * TILE : (c + 1) * TILE] = jnp.concatenate(rows, axis=0).astype(BF16)
            field[g] += dot(lhs[...], hot[j])
            return carry

        return lax.fori_loop(low, high, group_step, carry)

    lax.fori_loop(0, TILES, tile_step, 0)


def add_grad(keys_ref, resid, hot, grad):
    grad[...] = jnp.zeros_like(grad)

    def tile_step(j, carry):
        keys = keys_ref[j]
        low, high = group_range(keys)

        def group_step(g, carry):
            masks = group_masks(keys, g)
            rows = resid[g]
            for c in range(0, Q, 2):
                count = min(2, Q - c)
                part = hot[j, c * TILE : (c + count) * TILE, :]
                out = lax.dot_general(
                    rows, part, (((1,), (1,)), ((), ())), preferred_element_type=F32
                )
                for i in range(count):
                    total = grad[j, c + i]
                    for m in range(GROUP):
                        piece = out[m * QP : (m + 1) * QP, i * TILE : (i + 1) * TILE]
                        total = jnp.where(masks[m], piece, total)
                    grad[j, c + i] = total
            return carry

        return lax.fori_loop(low, high, group_step, carry)

    lax.fori_loop(0, TILES, tile_step, 0)


def own_field_kernel(
    alignment, pack, coup, states, hot, to_plain_out, keys_ref, field, sorted_blocks, blocks, lhs
):
    for n in range(RES // 256):
        rows = slice(n * 256, (n + 1) * 256)
        states[rows, :] = alignment[rows, :].astype(F32).astype(BF16)
    packed = pack[...]
    flipped = jnp.transpose(packed.astype(F32))
    to_sorted, to_plain, far, keys = order_half(packed, flipped, True)
    to_plain_out[...] = to_plain
    store_keys(keys, keys_ref)
    sorted_blocks[...] = jnp.zeros_like(sorted_blocks)
    ordered = dot(coup[...], to_sorted)
    for j in range(TILES):
        sorted_blocks[j, 0 : Q * Q, :] = ordered[:, j * TILE : (j + 1) * TILE]
    for c in range(Q):
        for j in range(TILES):
            blocks[j, c] = sorted_blocks[j, pl.ds(c, QP, stride=Q), :]
    fill_hot(far, states, hot)
    field[...] = jnp.zeros_like(field)
    add_field(keys_ref, blocks, hot, lhs, field)


def own_field(alignment, pack, coup):
    return pl.pallas_call(
        own_field_kernel,
        out_shape=(
            jax.ShapeDtypeStruct((RES, SEQ), BF16),
            jax.ShapeDtypeStruct((TILES, DEEP, SEQ), BF16),
            jax.ShapeDtypeStruct((PAIRS, PAIRS), BF16),
            jax.ShapeDtypeStruct((TILES, 8, TILE), F32),
            jax.ShapeDtypeStruct((GROUPS, GROWS, SEQ), F32),
        ),
        in_specs=[VMEM] * 3,
        out_specs=(VMEM,) * 5,
        scratch_shapes=[
            pltpu.VMEM((TILES, 512, TILE), F32),
            pltpu.VMEM((TILES, Q, QP, TILE), F32),
            pltpu.VMEM((GROWS, DEEP), BF16),
        ],
        compiler_params=PARAMS,
        cost_estimate=pl.CostEstimate(
            flops=20_000_000_000, bytes_accessed=10_000_000, transcendentals=0
        ),
        name="own_field",
    )(alignment, pack, coup)


def recv_kernel(
    ids, q0, q1, q2, q3, states, own, fields, weights,
    grad_out, resid_out, field_out,
    wide, sorted_blocks, blocks, hot, lhs, field, grad, keys_ref,
):
    for back, part in enumerate((q0, q1, q2, q3)):
        flipped = jnp.transpose(part[...].astype(F32))
        owner = lax.rem(ids[0] + (4 - back), 4)
        wide[pl.ds(pl.multiple_of(owner * QUARTER, 8), QUARTER), :] = flipped[0:QUARTER]
        if back == 0:
            first = flipped
    to_sorted, to_plain, far, keys = order_half(q0[...], first, False)
    store_keys(keys, keys_ref)
    sorted_blocks[PADQ:512, :] = jnp.zeros((512 - PADQ, PAIRS), F32)
    sorted_blocks[0:PADQ, :] = dot(wide[...].astype(BF16), to_sorted)
    for a in range(Q):
        for j in range(TILES):
            blocks[j, a] = sorted_blocks[a * Q : a * Q + QP, j * TILE : (j + 1) * TILE]
    fill_hot(far, states, hot)
    field[...] = own[...]
    add_field(keys_ref, blocks, hot, lhs, field)

    my_states = states[pl.ds(pl.multiple_of(ids[1] * RL, 16), RL), :].astype(F32)
    state = iota((QP, SEQ), 0)
    valid = state < Q
    state = state.astype(F32)
    weight = weights[...]
    lane = iota((QP, TILE), 1)
    field_part = jnp.zeros((QP, TILE), F32)
    for g in range(GROUPS):
        pieces = []
        for m in range(GROUP):
            r = g * GROUP + m
            logits = field[g, m * QP : (m + 1) * QP, :] + fields[:, r : r + 1]
            logits = jnp.where(valid, logits, -1e30)
            top = jnp.max(logits, axis=0, keepdims=True)
            raised = jnp.exp(logits - top)
            soft = raised / jnp.sum(raised, axis=0, keepdims=True)
            hot_own = jnp.where(state == my_states[r : r + 1], 1.0, 0.0)
            rounded = (weight * (soft - hot_own)).astype(BF16).astype(F32)
            pieces.append(rounded)
            field_part = jnp.where(lane == r, jnp.sum(rounded, axis=1, keepdims=True), field_part)
        resid_out[g] = jnp.concatenate(pieces, axis=0).astype(BF16)
    field_out[...] = field_part

    add_grad(keys_ref, resid_out, hot, grad)
    wide[Q * Q // 8 * 8 : PADQ, :] = jnp.zeros((PADQ - Q * Q // 8 * 8, PAIRS), F32)
    for a in range(Q):
        for j in range(TILES):
            wide[a * Q : (a + 1) * Q, j * TILE : (j + 1) * TILE] = grad[j, a, 0:Q]
    grad_out[...] = dot(wide[...].astype(BF16), to_plain).astype(BF16)


def recv_half(ids, parts, states, own, fields, weights):
    return pl.pallas_call(
        recv_kernel,
        out_shape=(
            jax.ShapeDtypeStruct((PADQ, PAIRS), BF16),
            jax.ShapeDtypeStruct((GROUPS, GROWS, SEQ), BF16),
            jax.ShapeDtypeStruct((QP, TILE), F32),
        ),
        in_specs=[SMEM] + [VMEM] * 8,
        out_specs=(VMEM,) * 3,
        scratch_shapes=[
            pltpu.VMEM((PADQ, PAIRS), F32),
            pltpu.VMEM((512, PAIRS), F32),
            pltpu.VMEM((TILES, Q, QP, TILE), F32),
            pltpu.VMEM((TILES, DEEP, SEQ), BF16),
            pltpu.VMEM((GROWS, DEEP), BF16),
            pltpu.VMEM((GROUPS, GROWS, SEQ), F32),
            pltpu.VMEM((TILES, Q, QP, TILE), F32),
            pltpu.VMEM((TILES, 8, TILE), F32),
        ],
        compiler_params=PARAMS,
        cost_estimate=pl.CostEstimate(
            flops=20_000_000_000, bytes_accessed=10_000_000, transcendentals=0
        ),
        name="recv_half",
    )(ids, *parts, states, own, fields, weights)


def own_grad_kernel(keys_ref, to_plain, hot, resid, grad_out, grad, wide):
    add_grad(keys_ref, resid, hot, grad)
    total = jnp.zeros((PADQ, PAIRS), F32)
    for j in range(TILES):
        wide[j, Q * Q // 8 * 8 : PADQ, :] = jnp.zeros((PADQ - Q * Q // 8 * 8, TILE), F32)
        for c in range(Q):
            wide[j, pl.ds(c, Q, stride=Q), :] = grad[j, c, 0:Q]
        total = total + dot(wide[j].astype(BF16), to_plain[j * TILE : (j + 1) * TILE, :])
    grad_out[...] = total.astype(BF16)


def own_grad(keys, to_plain, hot, resid):
    return pl.pallas_call(
        own_grad_kernel,
        out_shape=jax.ShapeDtypeStruct((PADQ, PAIRS), BF16),
        in_specs=[VMEM] * 4,
        out_specs=VMEM,
        scratch_shapes=[
            pltpu.VMEM((TILES, Q, QP, TILE), F32),
            pltpu.VMEM((TILES, PADQ, TILE), F32),
        ],
        compiler_params=PARAMS,
        cost_estimate=pl.CostEstimate(
            flops=12_000_000_000, bytes_accessed=8_000_000, transcendentals=0
        ),
        name="own_grad",
    )(keys, to_plain, hot, resid)


def back_kernel(mine, r1, r2, r3, out, tall):
    total = mine[...].astype(F32) + r1[...].astype(F32)
    total = total + (r2[...].astype(F32) + r3[...].astype(F32))
    tall[0:QUARTER, :] = total
    tall[QUARTER:TILE, :] = jnp.zeros((TILE - QUARTER, PAIRS), F32)
    out[...] = jnp.transpose(tall[...]).astype(BF16)


def sum_back(chunks):
    return pl.pallas_call(
        back_kernel,
        out_shape=jax.ShapeDtypeStruct((PAIRS, TILE), BF16),
        in_specs=[VMEM] * 4,
        out_specs=VMEM,
        scratch_shapes=[pltpu.VMEM((TILE, PAIRS), F32)],
        compiler_params=PARAMS,
        name="sum_back",
    )(*chunks)


def join_kernel(scale, mine, r1, r2, r3, remote, out):
    total = mine[...].astype(F32) + r1[...].astype(F32)
    total = total + (r2[...].astype(F32) + r3[...].astype(F32))
    flipped = jnp.transpose(remote[...].astype(F32))
    out[...] = (total + flipped[0:QUARTER]) * scale


def join_parts(scale, chunks, remote):
    return pl.pallas_call(
        functools.partial(join_kernel, scale),
        out_shape=jax.ShapeDtypeStruct((QUARTER, PAIRS), F32),
        in_specs=[VMEM] * 5,
        out_specs=VMEM,
        compiler_params=PARAMS,
        name="join_parts",
    )(*chunks, remote)


def place_kernel(scale, ids, c0, c1, c2, c3, f0, f1, f2, f3, out, field_out, wide):
    for back, part in enumerate((c0, c1, c2, c3)):
        owner = lax.rem(ids[0] + (4 - back), 4)
        wide[pl.ds(pl.multiple_of(owner * QUARTER, 8), QUARTER), :] = part[...]
    out[...] = wide[0 : Q * Q, :]
    field_out[...] = ((f0[...] + f1[...]) + (f2[...] + f3[...])) * scale


def place_parts(scale, ids, chunks, field_parts):
    return pl.pallas_call(
        functools.partial(place_kernel, scale),
        out_shape=(
            jax.ShapeDtypeStruct((Q * Q, PAIRS), F32),
            jax.ShapeDtypeStruct((QP, TILE), F32),
        ),
        in_specs=[SMEM] + [VMEM] * 8,
        out_specs=(VMEM, VMEM),
        scratch_shapes=[pltpu.VMEM((PADQ, PAIRS), F32)],
        compiler_params=PARAMS,
        name="place_parts",
    )(ids, *chunks, *field_parts)


def shifted(array, k):
    return lax.ppermute(array, "seq", [(i, (i + k) % 4) for i in range(4)])


def gather_seq(array):
    return [array] + [shifted(array, k) for k in (1, 2, 3)]


def scatter_seq(array, seq_index):
    def quarter(k):
        start = lax.rem(seq_index + k, 4) * QUARTER
        return lax.dynamic_slice_in_dim(array, start, QUARTER, 0)

    return [quarter(0)] + [shifted(quarter(k), k) for k in (1, 2, 3)]


def swap_blocks(array):
    blocks = array.reshape(BLOCKS, CAP, TILE)
    moved = lax.all_to_all(blocks, "res", split_axis=0, concat_axis=0, tiled=True)
    return moved.reshape(PAIRS, TILE)


def per_device(
    alignment, seq_weights, fields, couplings, pair_left, pair_slot, slot_residue, pair_count
):
    seq_index = lax.axis_index("seq")
    res_index = lax.axis_index("res")
    ids = jnp.stack([seq_index, res_index]).astype(jnp.int32)
    scale = Q / (SEQ * 4)
    coup = couplings.T
    table = jnp.concatenate(
        [slot_residue.reshape(BLOCKS, SLOTS).T, pair_count[None, :], jnp.zeros((3, BLOCKS), jnp.int32)]
    ).astype(BF16)
    pack = pack_pairs(ids, coup, pair_left[None, :], pair_slot[None, :], table)
    received = swap_blocks(pack)
    states, hot, to_plain, keys, field = own_field(alignment, pack, coup)
    parts = gather_seq(received)
    fields_t = jnp.pad(fields.T, ((0, QP - Q), (0, 0)))
    remote_grad, resid, field_part = recv_half(
        ids, parts, states, field, fields_t, seq_weights[None, :]
    )
    field_parts = gather_seq(field_part)
    remote_chunks = scatter_seq(remote_grad, seq_index)
    local_grad = own_grad(keys, to_plain, hot, resid)
    remote = swap_blocks(sum_back(remote_chunks))
    local_chunks = scatter_seq(local_grad, seq_index)
    joined = gather_seq(join_parts(scale, local_chunks, remote))
    coupling_grad, field_grad = place_parts(scale, ids, joined, field_parts)
    return coupling_grad.T, field_grad[:Q, :RL].T


def solution(mesh):
    in_specs = (
        P(None, "seq"),
        P("seq"),
        P("res", None),
        P("res", None),
        P("res"),
        P("res"),
        P("res"),
        P("res"),
    )
    out_specs = (P("res", None), P("res", None))
    return jax.shard_map(
        per_device, mesh=mesh, in_specs=in_specs, out_specs=out_specs, check_vma=False
    )
```

```python
import functools

import jax
import jax.numpy as jnp
from jax import lax
from jax.experimental import pallas as pl
from jax.experimental.pallas import tpu as pltpu
from jax.sharding import PartitionSpec as P

Q = 21
QP = 24
RL = 48
CAP = 8
SLOTS = 4
PAIRS = 512
BLOCKS = 64
SEQ = 256
RES = 3072
TILE = 128
TILES = PAIRS // TILE
GROUP = 8
GROUPS = RL // GROUP
GROWS = GROUP * QP
QUARTER = 112
PADQ = 4 * QUARTER
DEEP = Q * TILE
F32 = jnp.float32
BF16 = jnp.bfloat16
VMEM = pl.BlockSpec(memory_space=pltpu.VMEM)
SMEM = pl.BlockSpec(memory_space=pltpu.SMEM)
ANY = pl.BlockSpec(memory_space=pl.ANY)
PARAMS = pltpu.CompilerParams(vmem_limit_bytes=56 * 1024 * 1024)
SMALL = pltpu.CompilerParams(vmem_limit_bytes=16 * 1024 * 1024)
SENT = F32
SPANS = ((0, 6), (6, 12), (12, 18), (18, 21))


def iota(shape, dim):
    return lax.broadcasted_iota(jnp.int32, shape, dim)


def dot(x, y):
    return jnp.dot(x, y, preferred_element_type=F32)


def pack_kernel(coup, left, slot, residue, count, out, wide, tall):
    wide[...] = jnp.zeros_like(wide)
    wide[0 : Q * Q, :] = coup[...].astype(F32)
    start = pl.multiple_of(lax.axis_index("seq") * QUARTER, 8)
    tall[0:QUARTER, :] = wide[pl.ds(start, QUARTER), :]
    lane = iota((1, PAIRS), 1)
    bucket = lax.shift_right_logical(lane, 3)
    wanted = bucket * SLOTS + slot[...]
    pick = jnp.where(iota((BLOCKS * SLOTS, PAIRS), 0) == wanted, 1.0, 0.0).astype(BF16)
    partner = dot(jnp.broadcast_to(residue[...], (8, BLOCKS * SLOTS)).astype(F32).astype(BF16), pick)
    spread = jnp.where(iota((BLOCKS, PAIRS), 0) == bucket, 1.0, 0.0).astype(BF16)
    counts = dot(jnp.broadcast_to(count[...], (8, BLOCKS)).astype(F32).astype(BF16), spread)
    live = jnp.where((lane & (CAP - 1)).astype(F32) < counts[0:1], 1.0, 0.0)
    sub = iota((16, PAIRS), 0)
    index = jnp.where(sub == 0, left[...].astype(F32), 0.0)
    index = jnp.where(sub == 1, partner[0:1], index)
    index = jnp.where(sub == 2, live, index)
    index = jnp.where(sub == 3, lax.axis_index("res").astype(F32), index)
    index = jnp.where(sub == 4, bucket.astype(F32), index)
    tall[QUARTER:TILE, :] = index
    out[...] = jnp.transpose(tall[...]).astype(BF16)


def pack_pairs(coup, left, slot, residue, count):
    return pl.pallas_call(
        pack_kernel,
        out_shape=jax.ShapeDtypeStruct((PAIRS, TILE), BF16),
        in_specs=[VMEM] * 5,
        out_specs=VMEM,
        scratch_shapes=[pltpu.VMEM((PADQ, PAIRS), F32), pltpu.VMEM((TILE, PAIRS), F32)],
        compiler_params=PARAMS,
        name="pack_pairs",
    )(coup, left, slot, residue, count)


def order_half(pack, flipped, own):
    mine, other, block = (112, 113, 116) if own else (113, 112, 115)
    wide = pack.astype(F32)
    key_row = jnp.where(flipped[114:115] > 0.5, flipped[mine : mine + 1], float(RL))
    key_col = jnp.where(wide[:, 114:115] > 0.5, wide[:, mine : mine + 1], float(RL))
    lane = iota((PAIRS, PAIRS), 1).astype(F32)
    sub = iota((PAIRS, PAIRS), 0).astype(F32)
    full_row = key_row * PAIRS + lane
    full_col = key_col * PAIRS + sub
    place_row = jnp.sum(jnp.where(full_col < full_row, 1.0, 0.0), axis=0, keepdims=True)
    place_col = jnp.sum(jnp.where(full_row < full_col, 1.0, 0.0), axis=1, keepdims=True)
    to_sorted = jnp.where(place_col == lane, 1.0, 0.0).astype(BF16)
    to_plain = jnp.where(place_row == sub, 1.0, 0.0).astype(BF16)
    cols = dot(to_plain, pack)
    far = cols[:, block : block + 1] * RL + cols[:, other : other + 1]
    keys = dot(jnp.broadcast_to(key_row, (8, PAIRS)).astype(BF16), to_sorted)
    return to_sorted, place_row, far, keys


def plain_order(place):
    return jnp.where(place[0:1] == iota((PAIRS, PAIRS), 0).astype(F32), 1.0, 0.0).astype(BF16)


def sorted_order(place):
    col = jnp.transpose(jnp.broadcast_to(place[0:1], (TILE, PAIRS)))[:, 0:1]
    return jnp.where(col == iota((PAIRS, PAIRS), 1).astype(F32), 1.0, 0.0).astype(BF16)


def find_far(far, states):
    far_states = jnp.zeros((PAIRS, SEQ), F32)
    chunk = 256
    lane = iota((PAIRS, chunk), 1).astype(F32)
    for n in range(RES // chunk):
        pick = jnp.where(far - float(n * chunk) == lane, 1.0, 0.0).astype(BF16)
        far_states = far_states + dot(pick, states[n * chunk : (n + 1) * chunk, :])
    return far_states


def fill_hot(far_states, j, hot):
    tile = far_states[j * TILE : (j + 1) * TILE]
    for c in range(Q):
        hot[j, c * TILE : (c + 1) * TILE, :] = jnp.where(tile == float(c), 1.0, 0.0).astype(BF16)


def fill_flat(far_states, j, flat):
    tile = jnp.transpose(far_states[j * TILE : (j + 1) * TILE])
    for c in range(Q):
        flat[j, :, c * TILE : (c + 1) * TILE] = jnp.where(tile == float(c), 1.0, 0.0).astype(BF16)


def store_keys(keys, keys_ref):
    for j in range(TILES):
        keys_ref[j] = keys[:, j * TILE : (j + 1) * TILE]


def group_range(keys):
    low = jnp.min(keys).astype(jnp.int32)
    high = jnp.max(jnp.where(keys < RL - 0.5, keys, -1.0)).astype(jnp.int32)
    return low // GROUP, (high + GROUP) // GROUP


def group_masks(keys, g):
    base = (g * GROUP).astype(F32)
    wide = jnp.broadcast_to(keys[0:1], (QP, TILE))
    return [wide == base + float(m) for m in range(GROUP)]


def add_field(keys_ref, blocks, hot, lhs, field, wait=None):
    def tile_step(j, carry):
        if wait is not None:
            wait(j)
        keys = keys_ref[j]
        low, high = group_range(keys)

        def group_step(g, carry):
            masks = group_masks(keys, g)
            total = field[g]
            for n, (first, last) in enumerate(SPANS):
                for c in range(first, last):
                    block = blocks[j, c]
                    rows = [jnp.where(mask, block, 0.0) for mask in masks]
                    lhs[n][:, (c - first) * TILE : (c - first + 1) * TILE] = jnp.concatenate(
                        rows, axis=0
                    ).astype(BF16)
                total = total + dot(lhs[n][...], hot[j, first * TILE : last * TILE, :])
            field[g] = total
            return carry

        return lax.fori_loop(low, high, group_step, carry)

    lax.fori_loop(0, TILES, tile_step, 0)


def add_grad(keys_ref, resid, flat, grad, wait=None):
    grad[...] = jnp.zeros_like(grad)

    def tile_step(j, carry):
        if wait is not None:
            wait(j)
        keys = keys_ref[j]
        low, high = group_range(keys)

        def group_step(g, carry):
            masks = group_masks(keys, g)
            rows = resid[g]
            for c in range(0, Q, 2):
                count = min(2, Q - c)
                out = dot(rows, flat[j, :, c * TILE : (c + count) * TILE])
                for i in range(count):
                    total = grad[j, c + i]
                    for m in range(GROUP):
                        piece = out[m * QP : (m + 1) * QP, i * TILE : (i + 1) * TILE]
                        total = jnp.where(masks[m], piece, total)
                    grad[j, c + i] = total
            return carry

        return lax.fori_loop(low, high, group_step, carry)

    lax.fori_loop(0, TILES, tile_step, 0)


def store_quarters(full, outs):
    seq_index = lax.axis_index("seq")
    for k, out in enumerate(outs):
        owner = lax.rem(seq_index + k, 4)
        out[0:QUARTER, :] = full[pl.ds(pl.multiple_of(owner * QUARTER, 8), QUARTER), :].astype(BF16)


def own_field_kernel(
    alignment, pack, coup, states, far_out, place_out, keys_ref, field,
    sorted_blocks, blocks, hot, *lhs,
):
    for n in range(RES // 256):
        rows = slice(n * 256, (n + 1) * 256)
        states[rows, :] = alignment[rows, :].astype(F32).astype(BF16)
    packed = pack[...]
    flipped = jnp.transpose(packed.astype(F32))
    to_sorted, place, far, keys = order_half(packed, flipped, True)
    place_out[...] = jnp.broadcast_to(place, (8, PAIRS))
    store_keys(keys, keys_ref)
    sorted_blocks[...] = jnp.zeros_like(sorted_blocks)
    ordered = dot(coup[...], to_sorted)
    for j in range(TILES):
        sorted_blocks[j, 0 : Q * Q, :] = ordered[:, j * TILE : (j + 1) * TILE]
    for c in range(Q):
        for j in range(TILES):
            blocks[j, c] = sorted_blocks[j, pl.ds(c, QP, stride=Q), :]
    far_states = find_far(far, states)
    far_out[...] = far_states.astype(BF16)
    for j in range(TILES):
        fill_hot(far_states, j, hot)
    field[...] = jnp.zeros_like(field)
    add_field(keys_ref, blocks, hot, lhs, field)


def lhs_scratch():
    return [pltpu.VMEM((GROWS, (last - first) * TILE), BF16) for first, last in SPANS]


def own_field(alignment, pack, coup):
    return pl.pallas_call(
        own_field_kernel,
        out_shape=(
            jax.ShapeDtypeStruct((RES, SEQ), BF16),
            jax.ShapeDtypeStruct((PAIRS, SEQ), BF16),
            jax.ShapeDtypeStruct((8, PAIRS), F32),
            jax.ShapeDtypeStruct((TILES, 8, TILE), F32),
            jax.ShapeDtypeStruct((GROUPS, GROWS, SEQ), F32),
        ),
        in_specs=[VMEM] * 3,
        out_specs=(VMEM,) * 5,
        scratch_shapes=[
            pltpu.VMEM((TILES, 512, TILE), F32),
            pltpu.VMEM((TILES, Q, QP, TILE), F32),
            pltpu.VMEM((TILES, DEEP, SEQ), BF16),
        ]
        + lhs_scratch(),
        compiler_params=PARAMS,
        cost_estimate=pl.CostEstimate(
            flops=10_000_000_000, bytes_accessed=10_000_000, transcendentals=0
        ),
        name="own_field",
    )(alignment, pack, coup)


def recv_order_kernel(pack, states, far_out, place_out, keys_ref, codes):
    packed = pack[...]
    flipped = jnp.transpose(packed.astype(F32))
    to_sorted, place, far, keys = order_half(packed, flipped, False)
    store_keys(keys, keys_ref)
    place_out[...] = jnp.broadcast_to(place, (8, PAIRS))
    far_out[...] = find_far(far, states).astype(BF16)
    codes[...] = states[pl.ds(pl.multiple_of(lax.axis_index("res") * RL, 16), RL), :]


def recv_order(pack, states):
    return pl.pallas_call(
        recv_order_kernel,
        out_shape=(
            jax.ShapeDtypeStruct((PAIRS, SEQ), BF16),
            jax.ShapeDtypeStruct((8, PAIRS), F32),
            jax.ShapeDtypeStruct((TILES, 8, TILE), F32),
            jax.ShapeDtypeStruct((RL, SEQ), BF16),
        ),
        in_specs=[VMEM] * 2,
        out_specs=(VMEM,) * 4,
        compiler_params=PARAMS,
        cost_estimate=pl.CostEstimate(
            flops=5_000_000_000, bytes_accessed=3_000_000, transcendentals=0
        ),
        name="recv_order",
    )(pack, states)


def recv_kernel(
    q0, q1, q2, q3, far, place, keys_ref, codes, own, fields, weights,
    g0, g1, g2, g3, resid_out, field_out,
    wide, sorted_blocks, blocks, hot, flat, field, grad, *lhs,
):
    for back, part in enumerate((q0, q1, q2, q3)):
        flipped = jnp.transpose(part[...].astype(F32))
        owner = lax.rem(lax.axis_index("seq") + (4 - back), 4)
        wide[pl.ds(pl.multiple_of(owner * QUARTER, 8), QUARTER), :] = flipped[0:QUARTER]
    sorted_blocks[PADQ:512, :] = jnp.zeros((512 - PADQ, PAIRS), F32)
    sorted_blocks[0:PADQ, :] = dot(wide[...].astype(BF16), sorted_order(place))
    for a in range(Q):
        for j in range(TILES):
            blocks[j, a] = sorted_blocks[a * Q : a * Q + QP, j * TILE : (j + 1) * TILE]
    far_states = far[...].astype(F32)
    for j in range(TILES):
        fill_hot(far_states, j, hot)
    field[...] = own[...]
    add_field(keys_ref, blocks, hot, lhs, field)

    my_codes = codes[...].astype(F32)
    state = iota((QP, SEQ), 0).astype(F32)
    weight = weights[...]
    lane = iota((QP, TILE), 1)
    local = jnp.concatenate([fields[...], jnp.full((QP - Q, RL), -1e30, F32)], axis=0)
    for g in range(GROUPS):
        pieces = []
        for m in range(GROUP):
            r = g * GROUP + m
            logits = field[g, m * QP : (m + 1) * QP, :] + local[:, r : r + 1]
            top = jnp.max(logits, axis=0, keepdims=True)
            raised = jnp.exp(logits - top)
            share = weight / jnp.sum(raised, axis=0, keepdims=True)
            hot_own = jnp.where(state == my_codes[r : r + 1], weight, 0.0)
            pieces.append(raised * share - hot_own)
        resid_out[g] = jnp.concatenate(pieces, axis=0).astype(BF16)
    field_part = jnp.zeros((QP, TILE), F32)
    ones = jnp.ones((SEQ, TILE), BF16)
    for g in range(GROUPS):
        sums = dot(resid_out[g], ones)
        for m in range(GROUP):
            piece = sums[m * QP : (m + 1) * QP]
            field_part = jnp.where(lane == g * GROUP + m, piece, field_part)
    field_out[...] = field_part

    for j in range(TILES):
        fill_flat(far_states, j, flat)
    add_grad(keys_ref, resid_out, flat, grad)
    wide[Q * Q // 8 * 8 : PADQ, :] = jnp.zeros((PADQ - Q * Q // 8 * 8, PAIRS), F32)
    for a in range(Q):
        for j in range(TILES):
            wide[a * Q : (a + 1) * Q, j * TILE : (j + 1) * TILE] = grad[j, a, 0:Q]
    wide[...] = dot(wide[...].astype(BF16), plain_order(place))
    store_quarters(wide, (g0, g1, g2, g3))


def recv_half(parts, order, own, fields, weights):
    return pl.pallas_call(
        recv_kernel,
        out_shape=(jax.ShapeDtypeStruct((QUARTER, PAIRS), BF16),) * 4
        + (
            jax.ShapeDtypeStruct((GROUPS, GROWS, SEQ), BF16),
            jax.ShapeDtypeStruct((QP, TILE), F32),
        ),
        in_specs=[VMEM] * 11,
        out_specs=(VMEM,) * 6,
        scratch_shapes=[
            pltpu.VMEM((PADQ, PAIRS), F32),
            pltpu.VMEM((512, PAIRS), F32),
            pltpu.VMEM((TILES, Q, QP, TILE), F32),
            pltpu.VMEM((TILES, DEEP, SEQ), BF16),
            pltpu.VMEM((TILES, SEQ, DEEP), BF16),
            pltpu.VMEM((GROUPS, GROWS, SEQ), F32),
            pltpu.VMEM((TILES, Q, QP, TILE), F32),
        ]
        + lhs_scratch(),
        compiler_params=PARAMS,
        cost_estimate=pl.CostEstimate(
            flops=20_000_000_000, bytes_accessed=10_000_000, transcendentals=0
        ),
        name="recv_half",
    )(*parts, *order, own, fields, weights)


def own_grad_kernel(
    keys_ref, place, far, resid, field_part, g0, g1, g2, g3, grad, wide, full, flat
):
    far_states = far[...].astype(F32)
    for j in range(TILES):
        fill_flat(far_states, j, flat)
    add_grad(keys_ref, resid, flat, grad)
    to_plain = plain_order(place)
    total = jnp.zeros((PADQ, PAIRS), F32)
    for j in range(TILES):
        wide[j, Q * Q // 8 * 8 : PADQ, :] = jnp.zeros((PADQ - Q * Q // 8 * 8, TILE), F32)
        for c in range(Q):
            wide[j, pl.ds(c, Q, stride=Q), :] = grad[j, c, 0:Q]
        total = total + dot(wide[j].astype(BF16), to_plain[j * TILE : (j + 1) * TILE, :])
    full[...] = total
    outs = (g0, g1, g2, g3)
    store_quarters(full, outs)
    exact = field_part[...]
    coarse = exact.astype(BF16).astype(F32)
    rest = exact - coarse
    tail = jnp.concatenate(
        [coarse[0:16], jnp.concatenate([coarse[16:24], rest[0:8]], axis=0), rest[8:24],
         jnp.zeros((16, TILE), F32)], axis=1,
    ).astype(BF16)
    for out in outs:
        out[QUARTER:TILE, :] = tail


def own_grad(keys, place, far, resid, field_part):
    return pl.pallas_call(
        own_grad_kernel,
        out_shape=(jax.ShapeDtypeStruct((TILE, PAIRS), BF16),) * 4,
        in_specs=[VMEM] * 5,
        out_specs=(VMEM,) * 4,
        scratch_shapes=[
            pltpu.VMEM((TILES, Q, QP, TILE), F32),
            pltpu.VMEM((TILES, PADQ, TILE), F32),
            pltpu.VMEM((PADQ, PAIRS), F32),
            pltpu.VMEM((TILES, SEQ, DEEP), BF16),
        ],
        compiler_params=PARAMS,
        cost_estimate=pl.CostEstimate(
            flops=6_000_000_000, bytes_accessed=8_000_000, transcendentals=0
        ),
        name="own_grad",
    )(keys, place, far, resid, field_part)


def back_kernel(mine, r1, r2, r3, out, tall):
    total = mine[...].astype(F32) + r1[...].astype(F32)
    total = total + (r2[...].astype(F32) + r3[...].astype(F32))
    tall[0:QUARTER, :] = total
    tall[QUARTER:TILE, :] = jnp.zeros((TILE - QUARTER, PAIRS), F32)
    out[...] = jnp.transpose(tall[...]).astype(BF16)


def sum_back(chunks):
    return pl.pallas_call(
        back_kernel,
        out_shape=jax.ShapeDtypeStruct((PAIRS, TILE), BF16),
        in_specs=[VMEM] * 4,
        out_specs=VMEM,
        scratch_shapes=[pltpu.VMEM((TILE, PAIRS), F32)],
        compiler_params=SMALL,
        name="sum_back",
    )(*chunks)


def join_kernel(scale, mine, r1, r2, r3, remote, out, field_out):
    total = mine[...].astype(F32) + r1[...].astype(F32)
    total = total + (r2[...].astype(F32) + r3[...].astype(F32))
    flipped = jnp.transpose(remote[...].astype(F32))
    out[...] = (total[0:QUARTER] + flipped[0:QUARTER]) * scale
    tail = total[QUARTER:TILE]
    first = tail[:, 0:TILE]
    middle = tail[:, TILE : 2 * TILE]
    last = tail[:, 2 * TILE : 3 * TILE]
    coarse = jnp.concatenate([first, middle[0:8]], axis=0)
    rest = jnp.concatenate([middle[8:16], last], axis=0)
    field_out[...] = ((coarse + rest) * scale)[0:Q, 0:RL]


def join_parts(scale, chunks, remote):
    return pl.pallas_call(
        functools.partial(join_kernel, scale),
        out_shape=(
            jax.ShapeDtypeStruct((QUARTER, PAIRS), SENT),
            jax.ShapeDtypeStruct((Q, RL), F32),
        ),
        in_specs=[VMEM] * 5,
        out_specs=(VMEM, VMEM),
        compiler_params=SMALL,
        name="join_parts",
    )(*chunks, remote)


def place_kernel(c0, c1, c2, c3, out, wide):
    for back, part in enumerate((c0, c1, c2, c3)):
        owner = lax.rem(lax.axis_index("seq") + (4 - back), 4)
        wide[pl.ds(pl.multiple_of(owner * QUARTER, 8), QUARTER), :] = part[...].astype(F32)
    out[...] = wide[0 : Q * Q, :]


def place_parts(chunks):
    return pl.pallas_call(
        place_kernel,
        out_shape=jax.ShapeDtypeStruct((Q * Q, PAIRS), F32),
        in_specs=[VMEM] * 4,
        out_specs=VMEM,
        scratch_shapes=[pltpu.VMEM((PADQ, PAIRS), F32)],
        compiler_params=SMALL,
        name="place_parts",
    )(*chunks)


def shifted(array, k):
    return lax.ppermute(array, "seq", [(i, (i + k) % 4) for i in range(4)])


def gather_seq(array):
    return [array] + [shifted(array, k) for k in (1, 2, 3)]


def scatter_seq(quarters):
    return [quarters[0]] + [shifted(quarters[k], k) for k in (1, 2, 3)]


def swap_blocks(array):
    blocks = array.reshape(BLOCKS, CAP, TILE)
    moved = lax.all_to_all(blocks, "res", split_axis=0, concat_axis=0, tiled=True)
    return moved.reshape(PAIRS, TILE)


def per_device(
    alignment, seq_weights, fields, couplings, pair_left, pair_slot, slot_residue, pair_count
):
    scale = Q / (SEQ * 4)
    coup = couplings.T
    pack = pack_pairs(
        coup, pair_left[None, :], pair_slot[None, :], slot_residue[None, :], pair_count[None, :]
    )
    received = swap_blocks(pack)
    states, far, place, keys, field = own_field(alignment, pack, coup)
    received, field, states = lax.optimization_barrier((received, field, states))
    parts = gather_seq(received)
    order = recv_order(received, states)
    remote = recv_half(parts, order, field, fields.T, seq_weights[None, :])
    remote_quarters, resid, field_part = remote[:4], remote[4], remote[5]
    remote_chunks = scatter_seq(remote_quarters)
    local_quarters = own_grad(keys, place, far, resid, field_part)
    remote_chunks, local_quarters = lax.optimization_barrier((remote_chunks, local_quarters))
    swapped = swap_blocks(sum_back(remote_chunks))
    local_chunks = scatter_seq(local_quarters)
    joined, field_grad = join_parts(scale, local_chunks, swapped)
    coupling_grad = place_parts(gather_seq(joined))
    return coupling_grad.T, field_grad.T


def solution(mesh):
    in_specs = (
        P(None, "seq"),
        P("seq"),
        P("res", None),
        P("res", None),
        P("res"),
        P("res"),
        P("res"),
        P("res"),
    )
    out_specs = (P("res", None), P("res", None))
    return jax.shard_map(
        per_device, mesh=mesh, in_specs=in_specs, out_specs=out_specs, check_vma=False
    )
```

```python
import functools

import jax
import jax.numpy as jnp
from jax import lax
from jax.experimental import pallas as pl
from jax.experimental.pallas import tpu as pltpu
from jax.sharding import PartitionSpec as P

Q = 21
QP = 24
RL = 48
CAP = 8
SLOTS = 4
PAIRS = 512
BLOCKS = 64
SEQ = 256
RES = 3072
TILE = 128
WIDE = PAIRS // TILE
SPAN = 64
TILES = PAIRS // SPAN
DUOS = (Q + 1) // 2
GROUP = 8
GROUPS = RL // GROUP
GROWS = GROUP * QP
QUARTER = 112
PADQ = 4 * QUARTER
DEEP = DUOS * TILE
F32 = jnp.float32
BF16 = jnp.bfloat16
VMEM = pl.BlockSpec(memory_space=pltpu.VMEM)
SMEM = pl.BlockSpec(memory_space=pltpu.SMEM)
ANY = pl.BlockSpec(memory_space=pl.ANY)
PARAMS = pltpu.CompilerParams(vmem_limit_bytes=24 * 1024 * 1024)
LARGE = pltpu.CompilerParams(vmem_limit_bytes=56 * 1024 * 1024)
SMALL = pltpu.CompilerParams(vmem_limit_bytes=16 * 1024 * 1024)
SENT = BF16


def iota(shape, dim):
    return lax.broadcasted_iota(jnp.int32, shape, dim)


def dot(x, y):
    return jnp.dot(x, y, preferred_element_type=F32)


def pack_kernel(coup, left, slot, residue, count, out, wide):
    wide[...] = jnp.zeros_like(wide)
    wide[0 : Q * Q, :] = coup[...].astype(F32)
    lane = iota((1, PAIRS), 1)
    bucket = lax.shift_right_logical(lane, 3)
    wanted = bucket * SLOTS + slot[...]
    pick = jnp.where(iota((BLOCKS * SLOTS, PAIRS), 0) == wanted, 1.0, 0.0).astype(BF16)
    partner = dot(jnp.broadcast_to(residue[...], (8, BLOCKS * SLOTS)).astype(F32).astype(BF16), pick)
    spread = jnp.where(iota((BLOCKS, PAIRS), 0) == bucket, 1.0, 0.0).astype(BF16)
    counts = dot(jnp.broadcast_to(count[...], (8, BLOCKS)).astype(F32).astype(BF16), spread)
    live = jnp.where((lane & (CAP - 1)).astype(F32) < counts[0:1], 1.0, 0.0)
    sub = iota((16, PAIRS), 0)
    index = jnp.where(sub == 0, left[...].astype(F32), 0.0)
    index = jnp.where(sub == 1, partner[0:1], index)
    index = jnp.where(sub == 2, live, index)
    index = jnp.where(sub == 3, lax.axis_index("res").astype(F32), index)
    index = jnp.where(sub == 4, bucket.astype(F32), index)
    for n in range(4):
        part = jnp.concatenate([wide[n * QUARTER : (n + 1) * QUARTER, :], index], axis=0)
        out[:, n * TILE : (n + 1) * TILE] = jnp.transpose(part).astype(BF16)


def pack_pairs(coup, left, slot, residue, count):
    return pl.pallas_call(
        pack_kernel,
        out_shape=jax.ShapeDtypeStruct((PAIRS, 4 * TILE), BF16),
        in_specs=[VMEM] * 5,
        out_specs=VMEM,
        scratch_shapes=[pltpu.VMEM((PADQ, PAIRS), F32)],
        compiler_params=LARGE,
        name="pack_pairs",
    )(coup, left, slot, residue, count)


def order_half(pack, flipped, own):
    mine, other, block = (112, 113, 116) if own else (113, 112, 115)
    wide = pack.astype(F32)
    key_row = jnp.where(flipped[114:115] > 0.5, flipped[mine : mine + 1], float(RL))
    key_col = jnp.where(wide[:, 114:115] > 0.5, wide[:, mine : mine + 1], float(RL))
    lane = iota((PAIRS, PAIRS), 1).astype(F32)
    sub = iota((PAIRS, PAIRS), 0).astype(F32)
    full_row = key_row * PAIRS + lane
    full_col = key_col * PAIRS + sub
    place_row = jnp.sum(jnp.where(full_col < full_row, 1.0, 0.0), axis=0, keepdims=True)
    place_col = jnp.sum(jnp.where(full_row < full_col, 1.0, 0.0), axis=1, keepdims=True)
    to_sorted = jnp.where(place_col == lane, 1.0, 0.0).astype(BF16)
    to_plain = jnp.where(place_row == sub, 1.0, 0.0).astype(BF16)
    cols = dot(to_plain, pack)
    far = cols[:, block : block + 1] * RL + cols[:, other : other + 1]
    keys = dot(jnp.broadcast_to(key_row, (8, PAIRS)).astype(BF16), to_sorted)
    return to_sorted, place_row, far, keys


def plain_order(place):
    return jnp.where(place[0:1] == iota((PAIRS, PAIRS), 0).astype(F32), 1.0, 0.0).astype(BF16)


def sorted_order(place):
    col = jnp.transpose(jnp.broadcast_to(place[0:1], (TILE, PAIRS)))[:, 0:1]
    return jnp.where(col == iota((PAIRS, PAIRS), 1).astype(F32), 1.0, 0.0).astype(BF16)


def find_far(far, states):
    far_states = jnp.zeros((PAIRS, SEQ), F32)
    chunk = 256
    lane = iota((PAIRS, chunk), 1).astype(F32)
    for n in range(RES // chunk):
        pick = jnp.where(far - float(n * chunk) == lane, 1.0, 0.0).astype(BF16)
        far_states = far_states + dot(pick, states[n * chunk : (n + 1) * chunk, :])
    return far_states


def fill_hot(far, j, hot):
    tile = far[pl.ds(pl.multiple_of(j * SPAN, SPAN), SPAN), :].astype(F32)
    for c in range(2 * DUOS):
        hot[j, c * SPAN : (c + 1) * SPAN, :] = jnp.where(tile == float(c), 1.0, 0.0).astype(BF16)


def halves(first, second):
    low = iota(first.shape, 1) < SPAN
    return (
        jnp.where(low, first, pltpu.roll(second, SPAN, 1)),
        jnp.where(low, pltpu.roll(first, SPAN, 1), second),
    )


def store_keys(keys, keys_ref, bounds):
    for n in range(WIDE):
        part = keys[:, n * TILE : (n + 1) * TILE]
        for i, span in enumerate(halves(part, part)):
            j = 2 * n + i
            keys_ref[j] = span
            bounds[0, j], bounds[1, j] = group_range(span)


def store_blocks(block, n, blocks):
    for d in range(DUOS):
        second = block(2 * d + 1) if 2 * d + 1 < Q else jnp.zeros((QP, TILE), F32)
        blocks[2 * n, d], blocks[2 * n + 1, d] = halves(block(2 * d), second)


def load_grad(grad, n):
    columns = []
    for d in range(DUOS):
        columns.extend(halves(grad[2 * n, d], grad[2 * n + 1, d]))
    return columns[:Q]


def group_range(keys):
    low = jnp.min(keys).astype(jnp.int32)
    high = jnp.max(jnp.where(keys < RL - 0.5, keys, -1.0)).astype(jnp.int32)
    return low // GROUP, (high + GROUP) // GROUP


def group_masks(keys, g):
    base = (g * GROUP).astype(F32)
    wide = jnp.broadcast_to(keys[0:1], (QP, TILE))
    return [wide == base + float(m) for m in range(GROUP)]


def add_field(keys_ref, bounds, blocks, far, hot, lhs, field):
    def tile_step(j, carry):
        keys = keys_ref[j]
        low, high = bounds[0, j], bounds[1, j]

        @pl.when(low < high)
        def _():
            fill_hot(far, j, hot)

        def group_step(g, carry):
            masks = group_masks(keys, g)
            for d in range(DUOS):
                block = blocks[j, d]
                rows = [jnp.where(mask, block, 0.0) for mask in masks]
                lhs[:, d * TILE : (d + 1) * TILE] = jnp.concatenate(rows, axis=0).astype(BF16)
            field[g] += dot(lhs[...], hot[j])
            return carry

        return lax.fori_loop(low, high, group_step, carry)

    lax.fori_loop(0, TILES, tile_step, 0)


def add_grad(keys_ref, bounds, resid, hot, grad, far=None):
    grad[...] = jnp.zeros_like(grad)

    def tile_step(j, carry):
        keys = keys_ref[j]
        low, high = bounds[0, j], bounds[1, j]
        if far is not None:

            @pl.when(low < high)
            def _():
                fill_hot(far, j, hot)

        def group_step(g, carry):
            masks = group_masks(keys, g)
            rows = resid[g]
            for d in range(0, DUOS, 2):
                count = min(2, DUOS - d)
                part = hot[j, d * TILE : (d + count) * TILE, :]
                out = lax.dot_general(
                    rows, part, (((1,), (1,)), ((), ())), preferred_element_type=F32
                )
                for i in range(count):
                    total = grad[j, d + i]
                    for m in range(GROUP):
                        piece = out[m * QP : (m + 1) * QP, i * TILE : (i + 1) * TILE]
                        total = jnp.where(masks[m], piece, total)
                    grad[j, d + i] = total
            return carry

        return lax.fori_loop(low, high, group_step, carry)

    lax.fori_loop(0, TILES, tile_step, 0)


def store_quarters(full, outs):
    seq_index = lax.axis_index("seq")
    for k, out in enumerate(outs):
        owner = lax.rem(seq_index + k, 4)
        out[0:QUARTER, :] = full[pl.ds(pl.multiple_of(owner * QUARTER, 8), QUARTER), :].astype(BF16)


def own_field_kernel(
    alignment, pack, coup, states, far_out, place_out, keys_ref, bounds, field,
    sorted_blocks, blocks, hot, lhs,
):
    chunk = 512
    parts = [slice(n * chunk, (n + 1) * chunk) for n in range(RES // chunk)]
    packed = pack[:, 0:TILE]
    flipped = jnp.transpose(packed.astype(F32))
    to_sorted, place, far, keys = order_half(packed, flipped, True)
    place_out[...] = jnp.broadcast_to(place, (8, PAIRS))
    store_keys(keys, keys_ref, bounds)
    sorted_blocks[...] = jnp.zeros_like(sorted_blocks)
    ordered = dot(coup[...], to_sorted)
    for n in range(WIDE):
        sorted_blocks[n, 0 : Q * Q, :] = ordered[:, n * TILE : (n + 1) * TILE]
        store_blocks(lambda c: sorted_blocks[n, pl.ds(c, QP, stride=Q), :], n, blocks)
    field[...] = jnp.zeros_like(field)
    far_states = jnp.zeros((PAIRS, SEQ), F32)
    lane = iota((PAIRS, chunk), 1).astype(F32)
    for n, rows in enumerate(parts):
        part = alignment[rows, :].astype(F32).astype(BF16)
        states[rows, :] = part
        pick = jnp.where(far - float(n * chunk) == lane, 1.0, 0.0).astype(BF16)
        far_states = far_states + dot(pick, part)
    far_out[...] = far_states.astype(BF16)
    add_field(keys_ref, bounds, blocks, far_out, hot, lhs, field)


def own_field(alignment, pack, coup):
    return pl.pallas_call(
        own_field_kernel,
        out_shape=(
            jax.ShapeDtypeStruct((RES, SEQ), BF16),
            jax.ShapeDtypeStruct((PAIRS, SEQ), BF16),
            jax.ShapeDtypeStruct((8, PAIRS), F32),
            jax.ShapeDtypeStruct((TILES, 8, TILE), F32),
            jax.ShapeDtypeStruct((2, TILES), jnp.int32),
            jax.ShapeDtypeStruct((GROUPS, GROWS, SEQ), F32),
        ),
        in_specs=[VMEM, VMEM, VMEM],
        out_specs=(VMEM, VMEM, VMEM, VMEM, SMEM, VMEM),
        scratch_shapes=[
            pltpu.VMEM((WIDE, 512, TILE), F32),
            pltpu.VMEM((TILES, DUOS, QP, TILE), F32),
            pltpu.VMEM((TILES, DEEP, SEQ), BF16),
            pltpu.VMEM((GROWS, DEEP), BF16),
        ],
        compiler_params=PARAMS,
        cost_estimate=pl.CostEstimate(
            flops=10_000_000_000, bytes_accessed=10_000_000, transcendentals=0
        ),
        name="own_field",
    )(alignment, pack, coup)


def recv_order_kernel(pack, states, far_out, place_out, keys_ref, bounds, codes):
    packed = pack[:, 0:TILE]
    flipped = jnp.transpose(packed.astype(F32))
    to_sorted, place, far, keys = order_half(packed, flipped, False)
    store_keys(keys, keys_ref, bounds)
    place_out[...] = jnp.broadcast_to(place, (8, PAIRS))
    far_out[...] = find_far(far, states).astype(BF16)
    codes[...] = states[pl.ds(pl.multiple_of(lax.axis_index("res") * RL, 16), RL), :]


def recv_order(pack, states):
    return pl.pallas_call(
        recv_order_kernel,
        out_shape=(
            jax.ShapeDtypeStruct((PAIRS, SEQ), BF16),
            jax.ShapeDtypeStruct((8, PAIRS), F32),
            jax.ShapeDtypeStruct((TILES, 8, TILE), F32),
            jax.ShapeDtypeStruct((2, TILES), jnp.int32),
            jax.ShapeDtypeStruct((RL, SEQ), BF16),
        ),
        in_specs=[VMEM] * 2,
        out_specs=(VMEM, VMEM, VMEM, SMEM, VMEM),
        compiler_params=PARAMS,
        cost_estimate=pl.CostEstimate(
            flops=5_000_000_000, bytes_accessed=3_000_000, transcendentals=0
        ),
        name="recv_order",
    )(pack, states)


def recv_kernel(
    parts, far, place, keys_ref, bounds, codes, own, fields, weights,
    grad_out, resid_out, field_out,
    wide, sorted_blocks, blocks, hot, lhs, field, grad,
):
    for n in range(4):
        flipped = jnp.transpose(parts[:, n * TILE : (n + 1) * TILE].astype(F32))
        wide[n * QUARTER : (n + 1) * QUARTER, :] = flipped[0:QUARTER]
    sorted_blocks[PADQ:512, :] = jnp.zeros((512 - PADQ, PAIRS), F32)
    sorted_blocks[0:PADQ, :] = dot(wide[...].astype(BF16), sorted_order(place))
    for n in range(WIDE):
        lanes = slice(n * TILE, (n + 1) * TILE)
        store_blocks(lambda a: sorted_blocks[a * Q : a * Q + QP, lanes], n, blocks)
    field[...] = own[...]
    add_field(keys_ref, bounds, blocks, far, hot, lhs, field)

    my_codes = codes[...].astype(F32)
    state = iota((QP, SEQ), 0).astype(F32)
    weight = weights[...]
    lane = iota((QP, TILE), 1)
    local = jnp.concatenate([fields[...], jnp.full((QP - Q, RL), -1e30, F32)], axis=0)
    for g in range(GROUPS):
        pieces = []
        for m in range(GROUP):
            r = g * GROUP + m
            logits = field[g, m * QP : (m + 1) * QP, :] + local[:, r : r + 1]
            top = jnp.max(logits, axis=0, keepdims=True)
            raised = jnp.exp(logits - top)
            share = weight / jnp.sum(raised, axis=0, keepdims=True)
            hot_own = jnp.where(state == my_codes[r : r + 1], weight, 0.0)
            pieces.append(raised * share - hot_own)
        resid_out[g] = jnp.concatenate(pieces, axis=0).astype(BF16)
    field_part = jnp.zeros((QP, TILE), F32)
    ones = jnp.ones((SEQ, TILE), BF16)
    for g in range(GROUPS):
        sums = dot(resid_out[g], ones)
        for m in range(GROUP):
            piece = sums[m * QP : (m + 1) * QP]
            field_part = jnp.where(lane == g * GROUP + m, piece, field_part)
    field_out[...] = field_part

    add_grad(keys_ref, bounds, resid_out, hot, grad)
    wide[Q * Q // 8 * 8 : PADQ, :] = jnp.zeros((PADQ - Q * Q // 8 * 8, PAIRS), F32)
    for n in range(WIDE):
        for a, column in enumerate(load_grad(grad, n)):
            wide[a * Q : (a + 1) * Q, n * TILE : (n + 1) * TILE] = column[0:Q]
    plain = dot(wide[...].astype(BF16), plain_order(place))
    rest = jnp.zeros((TILE - QUARTER, PAIRS), F32)
    for n in range(4):
        part = jnp.concatenate([plain[n * QUARTER : (n + 1) * QUARTER], rest], axis=0)
        grad_out[n] = jnp.transpose(part).astype(BF16)


def recv_half(received, order, own, fields, weights):
    return pl.pallas_call(
        recv_kernel,
        out_shape=(
            jax.ShapeDtypeStruct((4, PAIRS, TILE), BF16),
            jax.ShapeDtypeStruct((GROUPS, GROWS, SEQ), BF16),
            jax.ShapeDtypeStruct((QP, TILE), F32),
        ),
        in_specs=[VMEM] * 4 + [SMEM] + [VMEM] * 4,
        out_specs=(VMEM,) * 3,
        scratch_shapes=[
            pltpu.VMEM((PADQ, PAIRS), F32),
            pltpu.VMEM((512, PAIRS), F32),
            pltpu.VMEM((TILES, DUOS, QP, TILE), F32),
            pltpu.VMEM((TILES, DEEP, SEQ), BF16),
            pltpu.VMEM((GROWS, DEEP), BF16),
            pltpu.VMEM((GROUPS, GROWS, SEQ), F32),
            pltpu.VMEM((TILES, DUOS, QP, TILE), F32),
        ],
        compiler_params=PARAMS,
        cost_estimate=pl.CostEstimate(
            flops=20_000_000_000, bytes_accessed=10_000_000, transcendentals=0
        ),
        name="recv_half",
    )(received, *order, own, fields, weights)


def own_grad_kernel(
    keys_ref, bounds, place, far, resid, field_part, g0, g1, g2, g3, grad, wide, full, hot
):
    add_grad(keys_ref, bounds, resid, hot, grad, far)
    to_plain = plain_order(place)
    total = jnp.zeros((PADQ, PAIRS), F32)
    for n in range(WIDE):
        wide[n, Q * Q // 8 * 8 : PADQ, :] = jnp.zeros((PADQ - Q * Q // 8 * 8, TILE), F32)
        for c, column in enumerate(load_grad(grad, n)):
            wide[n, pl.ds(c, Q, stride=Q), :] = column[0:Q]
        total = total + dot(wide[n].astype(BF16), to_plain[n * TILE : (n + 1) * TILE, :])
    full[...] = total
    outs = (g0, g1, g2, g3)
    store_quarters(full, outs)
    exact = field_part[...]
    coarse = exact.astype(BF16).astype(F32)
    rest = exact - coarse
    tail = jnp.concatenate(
        [coarse[0:16], jnp.concatenate([coarse[16:24], rest[0:8]], axis=0), rest[8:24],
         jnp.zeros((16, TILE), F32)], axis=1,
    ).astype(BF16)
    for out in outs:
        out[QUARTER:TILE, :] = tail


def own_grad(keys, bounds, place, far, resid, field_part):
    return pl.pallas_call(
        own_grad_kernel,
        out_shape=(jax.ShapeDtypeStruct((TILE, PAIRS), BF16),) * 4,
        in_specs=[VMEM, SMEM] + [VMEM] * 4,
        out_specs=(VMEM,) * 4,
        scratch_shapes=[
            pltpu.VMEM((TILES, DUOS, QP, TILE), F32),
            pltpu.VMEM((WIDE, PADQ, TILE), F32),
            pltpu.VMEM((PADQ, PAIRS), F32),
            pltpu.VMEM((TILES, DEEP, SEQ), BF16),
        ],
        compiler_params=PARAMS,
        cost_estimate=pl.CostEstimate(
            flops=6_000_000_000, bytes_accessed=8_000_000, transcendentals=0
        ),
        name="own_grad",
    )(keys, bounds, place, far, resid, field_part)


def join_kernel(scale, mine, r1, r2, r3, remote, out, field_out):
    total = mine[...].astype(F32) + r1[...].astype(F32)
    total = total + (r2[...].astype(F32) + r3[...].astype(F32))
    summed = remote[0].astype(F32) + remote[1].astype(F32)
    summed = summed + (remote[2].astype(F32) + remote[3].astype(F32))
    flipped = jnp.transpose(summed)
    out[...] = ((total[0:QUARTER] + flipped[0:QUARTER]) * scale).astype(SENT)
    tail = total[QUARTER:TILE]
    first = tail[:, 0:TILE]
    middle = tail[:, TILE : 2 * TILE]
    last = tail[:, 2 * TILE : 3 * TILE]
    coarse = jnp.concatenate([first, middle[0:8]], axis=0)
    rest = jnp.concatenate([middle[8:16], last], axis=0)
    field_out[...] = ((coarse + rest) * scale)[0:Q, 0:RL]


def join_parts(scale, chunks, remote):
    return pl.pallas_call(
        functools.partial(join_kernel, scale),
        out_shape=(
            jax.ShapeDtypeStruct((QUARTER, PAIRS), SENT),
            jax.ShapeDtypeStruct((Q, RL), F32),
        ),
        in_specs=[VMEM] * 5,
        out_specs=(VMEM, VMEM),
        compiler_params=SMALL,
        name="join_parts",
    )(*chunks, remote)


def place_kernel(c0, c1, c2, c3, out, wide):
    for back, part in enumerate((c0, c1, c2, c3)):
        owner = lax.rem(lax.axis_index("seq") + (4 - back), 4)
        wide[pl.ds(pl.multiple_of(owner * QUARTER, 8), QUARTER), :] = part[...].astype(F32)
    out[...] = wide[0 : Q * Q, :]


def place_parts(chunks):
    return pl.pallas_call(
        place_kernel,
        out_shape=jax.ShapeDtypeStruct((Q * Q, PAIRS), F32),
        in_specs=[VMEM] * 4,
        out_specs=VMEM,
        scratch_shapes=[pltpu.VMEM((PADQ, PAIRS), F32)],
        compiler_params=SMALL,
        name="place_parts",
    )(*chunks)


def shifted(array, k):
    return lax.ppermute(array, "seq", [(i, (i + k) % 4) for i in range(4)])


def gather_seq(array):
    return [array] + [shifted(array, k) for k in (1, 2, 3)]


def scatter_seq(quarters):
    return [quarters[0]] + [shifted(quarters[k], k) for k in (1, 2, 3)]


def swap_blocks(array):
    blocks = array.reshape(BLOCKS, CAP, array.shape[1])
    moved = lax.all_to_all(blocks, "res", split_axis=0, concat_axis=0, tiled=True)
    return moved.reshape(array.shape)


def swap_quarters(array):
    blocks = array.reshape(4 * BLOCKS, CAP, TILE)
    moved = lax.all_to_all(blocks, ("seq", "res"), split_axis=0, concat_axis=0, tiled=True)
    return moved.reshape(4, PAIRS, TILE)


def per_device(
    alignment, seq_weights, fields, couplings, pair_left, pair_slot, slot_residue, pair_count
):
    scale = Q / (SEQ * 4)
    coup = couplings.T
    pack = pack_pairs(
        coup, pair_left[None, :], pair_slot[None, :], slot_residue[None, :], pair_count[None, :]
    )
    received = swap_blocks(pack)
    states, far, place, keys, bounds, field = own_field(alignment, pack, coup)
    received, field, states = lax.optimization_barrier((received, field, states))
    order = recv_order(received, states)
    remote_grad, resid, field_part = recv_half(received, order, field, fields.T, seq_weights[None, :])
    swapped = swap_quarters(remote_grad)
    local_quarters = own_grad(keys, bounds, place, far, resid, field_part)
    local_chunks = scatter_seq(local_quarters)
    joined, field_grad = join_parts(scale, local_chunks, swapped)
    coupling_grad = place_parts(gather_seq(joined))
    return coupling_grad.T, field_grad.T


def solution(mesh):
    in_specs = (
        P(None, "seq"),
        P("seq"),
        P("res", None),
        P("res", None),
        P("res"),
        P("res"),
        P("res"),
        P("res"),
    )
    out_specs = (P("res", None), P("res", None))
    return jax.shard_map(
        per_device, mesh=mesh, in_specs=in_specs, out_specs=out_specs, check_vma=False
    )
```

```python
import functools

import jax
import jax.numpy as jnp
from jax import lax
from jax.experimental import pallas as pl
from jax.experimental.pallas import tpu as pltpu
from jax.sharding import PartitionSpec as P

Q = 21
QP = 24
RL = 48
CAP = 8
SLOTS = 4
PAIRS = 512
BLOCKS = 64
SEQ = 256
RES = 3072
TILE = 128
WIDE = PAIRS // TILE
SPAN = 64
TILES = PAIRS // SPAN
DUOS = (Q + 1) // 2
ROWS = RL * QP
WINDOW = 16
WROWS = WINDOW * QP
QUARTER = 112
PADQ = 4 * QUARTER
DEEP = DUOS * TILE
F32 = jnp.float32
BF16 = jnp.bfloat16
VMEM = pl.BlockSpec(memory_space=pltpu.VMEM)
SMEM = pl.BlockSpec(memory_space=pltpu.SMEM)
PARAMS = pltpu.CompilerParams(vmem_limit_bytes=20 * 1024 * 1024)
LARGE = pltpu.CompilerParams(vmem_limit_bytes=56 * 1024 * 1024)
SMALL = pltpu.CompilerParams(vmem_limit_bytes=16 * 1024 * 1024)
SENT = BF16


def iota(shape, dim):
    return lax.broadcasted_iota(jnp.int32, shape, dim)


def dot(x, y):
    return jnp.dot(x, y, preferred_element_type=F32)


def pack_kernel(coup, left, slot, residue, count, out, wide):
    wide[...] = jnp.zeros_like(wide)
    wide[0 : Q * Q, :] = coup[...].astype(F32)
    lane = iota((1, PAIRS), 1)
    bucket = lax.shift_right_logical(lane, 3)
    wanted = bucket * SLOTS + slot[...]
    pick = jnp.where(iota((BLOCKS * SLOTS, PAIRS), 0) == wanted, 1.0, 0.0).astype(BF16)
    partner = dot(jnp.broadcast_to(residue[...], (8, BLOCKS * SLOTS)).astype(F32).astype(BF16), pick)
    spread = jnp.where(iota((BLOCKS, PAIRS), 0) == bucket, 1.0, 0.0).astype(BF16)
    counts = dot(jnp.broadcast_to(count[...], (8, BLOCKS)).astype(F32).astype(BF16), spread)
    live = jnp.where((lane & (CAP - 1)).astype(F32) < counts[0:1], 1.0, 0.0)
    sub = iota((16, PAIRS), 0)
    index = jnp.where(sub == 0, left[...].astype(F32), 0.0)
    index = jnp.where(sub == 1, partner[0:1], index)
    index = jnp.where(sub == 2, live, index)
    index = jnp.where(sub == 3, lax.axis_index("res").astype(F32), index)
    index = jnp.where(sub == 4, bucket.astype(F32), index)
    for n in range(4):
        part = jnp.concatenate([wide[n * QUARTER : (n + 1) * QUARTER, :], index], axis=0)
        out[:, n * TILE : (n + 1) * TILE] = jnp.transpose(part).astype(BF16)


def pack_pairs(coup, left, slot, residue, count):
    return pl.pallas_call(
        pack_kernel,
        out_shape=jax.ShapeDtypeStruct((PAIRS, 4 * TILE), BF16),
        in_specs=[VMEM] * 5,
        out_specs=VMEM,
        scratch_shapes=[pltpu.VMEM((PADQ, PAIRS), F32)],
        compiler_params=LARGE,
        name="pack_pairs",
    )(coup, left, slot, residue, count)


def order_half(pack, flipped, own):
    mine, other, block = (112, 113, 116) if own else (113, 112, 115)
    wide = pack.astype(F32)
    key_row = jnp.where(flipped[114:115] > 0.5, flipped[mine : mine + 1], float(RL))
    key_col = jnp.where(wide[:, 114:115] > 0.5, wide[:, mine : mine + 1], float(RL))
    lane = iota((PAIRS, PAIRS), 1).astype(F32)
    sub = iota((PAIRS, PAIRS), 0).astype(F32)
    full_row = key_row * PAIRS + lane
    full_col = key_col * PAIRS + sub
    place_row = jnp.sum(jnp.where(full_col < full_row, 1.0, 0.0), axis=0, keepdims=True)
    place_col = jnp.sum(jnp.where(full_row < full_col, 1.0, 0.0), axis=1, keepdims=True)
    to_sorted = jnp.where(place_col == lane, 1.0, 0.0).astype(BF16)
    to_plain = jnp.where(place_row == sub, 1.0, 0.0).astype(BF16)
    far = wide[:, block : block + 1] * RL + wide[:, other : other + 1]
    keys = dot(jnp.broadcast_to(key_row, (8, PAIRS)).astype(BF16), to_sorted)
    return to_sorted, to_plain, place_row, far, keys


def plain_order(place):
    return jnp.where(place[0:1] == iota((PAIRS, PAIRS), 0).astype(F32), 1.0, 0.0).astype(BF16)


def find_far(far, states, to_plain, plain):
    count = 5
    for start in range(0, BLOCKS, count):
        blocks = min(count, BLOCKS - start)
        pairs = slice(start * CAP, (start + blocks) * CAP)
        base = start * RL
        depth = min(256, RES - base)
        lane = iota((blocks * CAP, depth), 1).astype(F32)
        pick = jnp.where(far[pairs] - float(base) == lane, 1.0, 0.0).astype(BF16)
        plain[pairs, :] = dot(pick, states[base : base + depth, :])
    return dot(to_plain, plain[...].astype(BF16))


def fill_hot(far, j, hot):
    tile = far[pl.ds(pl.multiple_of(j * SPAN, SPAN), SPAN), :].astype(F32)
    for c in range(2 * DUOS):
        hot[j, c * SPAN : (c + 1) * SPAN, :] = jnp.where(tile == float(c), 1.0, 0.0).astype(BF16)


def halves(first, second):
    low = iota(first.shape, 1) < SPAN
    return (
        jnp.where(low, first, pltpu.roll(second, SPAN, 1)),
        jnp.where(low, pltpu.roll(first, SPAN, 1), second),
    )


def store_keys(keys, keys_ref, bounds):
    for n in range(WIDE):
        part = keys[:, n * TILE : (n + 1) * TILE]
        for i, span in enumerate(halves(part, part)):
            j = 2 * n + i
            keys_ref[j] = span
            bounds[0, j], bounds[1, j] = window_range(span)


def store_blocks(block, n, blocks):
    for d in range(DUOS):
        second = block(2 * d + 1) if 2 * d + 1 < Q else jnp.zeros((QP, TILE), F32)
        blocks[2 * n, d], blocks[2 * n + 1, d] = halves(block(2 * d), second)


def load_grad(grad, n):
    columns = []
    for d in range(DUOS):
        columns.extend(halves(grad[2 * n, d], grad[2 * n + 1, d]))
    return columns[:Q]


def window_range(keys):
    low = jnp.min(keys).astype(jnp.int32)
    high = jnp.max(jnp.where(keys < RL - 0.5, keys, -1.0)).astype(jnp.int32)
    first = low - (low & 1)
    return first, jnp.where(high >= 0, (high - first) // WINDOW + 1, 0)


def window_at(keys, first, step):
    start = first + step * WINDOW
    base = jnp.minimum(start, RL - WINDOW)
    fresh = jnp.where(keys[0:1] >= start.astype(F32), keys[0:1], -1.0)
    wide = jnp.broadcast_to(fresh, (QP, TILE))
    rows = pl.ds(pl.multiple_of(base * QP, 2 * QP), WROWS)
    return rows, [wide == (base + m).astype(F32) for m in range(WINDOW)]


def add_field(keys_ref, bounds, blocks, far, hot, lhs, field):
    def tile_step(j, carry):
        keys = keys_ref[j]
        first, count = bounds[0, j], bounds[1, j]

        @pl.when(count > 0)
        def _():
            fill_hot(far, j, hot)

        def window_step(step, carry):
            window, masks = window_at(keys, first, step)
            for d in range(DUOS):
                block = blocks[j, d]
                rows = [jnp.where(mask, block, 0.0) for mask in masks]
                lhs[:, d * TILE : (d + 1) * TILE] = jnp.concatenate(rows, axis=0).astype(BF16)
            field[window, :] += dot(lhs[...], hot[j])
            return carry

        return lax.fori_loop(0, count, window_step, carry)

    lax.fori_loop(0, TILES, tile_step, 0)


def add_grad(keys_ref, bounds, resid, hot, grad, far=None):
    grad[...] = jnp.zeros_like(grad)

    def tile_step(j, carry):
        keys = keys_ref[j]
        first, count = bounds[0, j], bounds[1, j]
        if far is not None:

            @pl.when(count > 0)
            def _():
                fill_hot(far, j, hot)

        def window_step(step, carry):
            window, masks = window_at(keys, first, step)
            rows = resid[window, :]
            for d in range(0, DUOS, 2):
                duos = min(2, DUOS - d)
                part = hot[j, d * TILE : (d + duos) * TILE, :]
                out = lax.dot_general(
                    rows, part, (((1,), (1,)), ((), ())), preferred_element_type=F32
                )
                for i in range(duos):
                    total = grad[j, d + i]
                    for m in range(WINDOW):
                        piece = out[m * QP : (m + 1) * QP, i * TILE : (i + 1) * TILE]
                        total = jnp.where(masks[m], piece, total)
                    grad[j, d + i] = total
            return carry

        return lax.fori_loop(0, count, window_step, carry)

    lax.fori_loop(0, TILES, tile_step, 0)


def store_quarters(full, outs):
    seq_index = lax.axis_index("seq")
    for k, out in enumerate(outs):
        owner = lax.rem(seq_index + k, 4)
        out[0:QUARTER, :] = full[pl.ds(pl.multiple_of(owner * QUARTER, 8), QUARTER), :].astype(BF16)


def own_field_kernel(
    alignment, pack, coup, states, far_out, place_out, keys_ref, bounds, field,
    sorted_blocks, blocks, hot, lhs, codes, plain,
):
    chunk = 512
    parts = [slice(n * chunk, (n + 1) * chunk) for n in range(RES // chunk)]
    packed = pack[:, 0:TILE]
    flipped = jnp.transpose(packed.astype(F32))
    to_sorted, to_plain, place, far, keys = order_half(packed, flipped, True)
    place_out[...] = jnp.broadcast_to(place, (8, PAIRS))
    store_keys(keys, keys_ref, bounds)
    sorted_blocks[...] = jnp.zeros_like(sorted_blocks)
    ordered = dot(coup[...], to_sorted)
    for n in range(WIDE):
        sorted_blocks[n, 0 : Q * Q, :] = ordered[:, n * TILE : (n + 1) * TILE]
        store_blocks(lambda c: sorted_blocks[n, pl.ds(c, QP, stride=Q), :], n, blocks)
    field[...] = jnp.zeros_like(field)
    for rows in parts:
        states[rows, :] = alignment[rows, :].astype(F32).astype(BF16)
    far_states = find_far(far, states, to_plain, plain)
    far_out[...] = far_states.astype(jnp.int8)
    codes[...] = far_states.astype(BF16)
    add_field(keys_ref, bounds, blocks, codes, hot, lhs, field)


def own_field(alignment, pack, coup):
    return pl.pallas_call(
        own_field_kernel,
        out_shape=(
            jax.ShapeDtypeStruct((RES, SEQ), BF16),
            jax.ShapeDtypeStruct((PAIRS, SEQ), jnp.int8),
            jax.ShapeDtypeStruct((8, PAIRS), F32),
            jax.ShapeDtypeStruct((TILES, 8, TILE), F32),
            jax.ShapeDtypeStruct((2, TILES), jnp.int32),
            jax.ShapeDtypeStruct((ROWS, SEQ), F32),
        ),
        in_specs=[VMEM, VMEM, VMEM],
        out_specs=(VMEM, VMEM, VMEM, VMEM, SMEM, VMEM),
        scratch_shapes=[
            pltpu.VMEM((WIDE, 512, TILE), F32),
            pltpu.VMEM((TILES, DUOS, QP, TILE), F32),
            pltpu.VMEM((TILES, DEEP, SEQ), BF16),
            pltpu.VMEM((WROWS, DEEP), BF16),
            pltpu.VMEM((PAIRS, SEQ), BF16),
            pltpu.VMEM((PAIRS, SEQ), F32),
        ],
        compiler_params=PARAMS,
        cost_estimate=pl.CostEstimate(
            flops=10_000_000_000, bytes_accessed=10_000_000, transcendentals=0
        ),
        name="own_field",
    )(alignment, pack, coup)


def recv_kernel(
    parts, states, own, fields, weights,
    grad_out, resid_out, field_out,
    wide, sorted_blocks, blocks, hot, lhs, field, grad, far, plain, keys_ref, bounds,
):
    packed = parts[:, 0:TILE]
    flipped = jnp.transpose(packed.astype(F32))
    to_sorted, to_plain, place, far_col, keys = order_half(packed, flipped, False)
    store_keys(keys, keys_ref, bounds)
    far[...] = find_far(far_col, states, to_plain, plain).astype(BF16)
    for n in range(4):
        if n > 0:
            flipped = jnp.transpose(parts[:, n * TILE : (n + 1) * TILE].astype(F32))
        wide[n * QUARTER : (n + 1) * QUARTER, :] = flipped[0:QUARTER]
    sorted_blocks[PADQ:512, :] = jnp.zeros((512 - PADQ, PAIRS), F32)
    sorted_blocks[0:PADQ, :] = dot(wide[0:PADQ, :].astype(BF16), to_sorted)
    for n in range(WIDE):
        lanes = slice(n * TILE, (n + 1) * TILE)
        store_blocks(lambda a: sorted_blocks[a * Q : a * Q + QP, lanes], n, blocks)
    field[...] = own[...]
    add_field(keys_ref, bounds, blocks, far, hot, lhs, field)

    mine = pl.ds(pl.multiple_of(lax.axis_index("res") * RL, 16), RL)
    my_codes = states[mine, :].astype(F32)
    state = iota((QP, SEQ), 0).astype(F32)
    weight = weights[...]
    lane = iota((QP, TILE), 1)
    local = jnp.concatenate([fields[...], jnp.full((QP - Q, RL), -1e30, F32)], axis=0)
    field_part = jnp.zeros((QP, TILE), F32)
    ones = jnp.ones((SEQ, TILE), BF16)
    for r in range(0, RL, 2):
        pieces = []
        for m in (r, r + 1):
            logits = field[m * QP : (m + 1) * QP, :] + local[:, m : m + 1]
            top = jnp.max(logits, axis=0, keepdims=True)
            raised = jnp.exp(logits - top)
            share = weight / jnp.sum(raised, axis=0, keepdims=True)
            hot_own = jnp.where(state == my_codes[m : m + 1], weight, 0.0)
            pieces.append(raised * share - hot_own)
        resid_out[r * QP : (r + 2) * QP, :] = jnp.concatenate(pieces, axis=0).astype(BF16)
    sums = dot(resid_out[...], ones)
    for r in range(RL):
        field_part = jnp.where(lane == r, sums[r * QP : (r + 1) * QP], field_part)
    field_out[...] = field_part

    add_grad(keys_ref, bounds, resid_out, hot, grad)
    for n in range(4):
        wide[n * TILE + QUARTER : (n + 1) * TILE, :] = jnp.zeros((TILE - QUARTER, PAIRS), F32)
    last = 3 * TILE + Q * Q - 3 * QUARTER
    wide[last // 8 * 8 : 3 * TILE + QUARTER, :] = jnp.zeros((3 * TILE + QUARTER - last // 8 * 8, PAIRS), F32)
    for n in range(WIDE):
        lanes = slice(n * TILE, (n + 1) * TILE)
        for a, column in enumerate(load_grad(grad, n)):
            done = 0
            while done < Q:
                quarter, row = divmod(a * Q + done, QUARTER)
                size = min(Q - done, QUARTER - row)
                start = quarter * TILE + row
                wide[start : start + size, lanes] = column[done : done + size]
                done += size
    result = lax.dot_general(
        to_sorted, wide[...].astype(BF16), (((1,), (1,)), ((), ())), preferred_element_type=F32
    )
    for n in range(4):
        grad_out[n] = result[:, n * TILE : (n + 1) * TILE].astype(BF16)


def recv_half(received, states, own, fields, weights):
    return pl.pallas_call(
        recv_kernel,
        out_shape=(
            jax.ShapeDtypeStruct((4, PAIRS, TILE), BF16),
            jax.ShapeDtypeStruct((ROWS, SEQ), BF16),
            jax.ShapeDtypeStruct((QP, TILE), F32),
        ),
        in_specs=[VMEM] * 5,
        out_specs=(VMEM,) * 3,
        scratch_shapes=[
            pltpu.VMEM((4 * TILE, PAIRS), F32),
            pltpu.VMEM((512, PAIRS), F32),
            pltpu.VMEM((TILES, DUOS, QP, TILE), F32),
            pltpu.VMEM((TILES, DEEP, SEQ), BF16),
            pltpu.VMEM((WROWS, DEEP), BF16),
            pltpu.VMEM((ROWS, SEQ), F32),
            pltpu.VMEM((TILES, DUOS, QP, TILE), F32),
            pltpu.VMEM((PAIRS, SEQ), BF16),
            pltpu.VMEM((PAIRS, SEQ), F32),
            pltpu.VMEM((TILES, 8, TILE), F32),
            pltpu.SMEM((2, TILES), jnp.int32),
        ],
        compiler_params=PARAMS,
        cost_estimate=pl.CostEstimate(
            flops=20_000_000_000, bytes_accessed=10_000_000, transcendentals=0
        ),
        name="recv_half",
    )(received, states, own, fields, weights)


def own_grad_kernel(
    keys_ref, bounds, place, far, resid, field_part, g0, g1, g2, g3, grad, wide, full, hot
):
    add_grad(keys_ref, bounds, resid, hot, grad, far)
    to_plain = plain_order(place)
    total = jnp.zeros((PADQ, PAIRS), F32)
    for n in range(WIDE):
        wide[n, Q * Q // 8 * 8 : PADQ, :] = jnp.zeros((PADQ - Q * Q // 8 * 8, TILE), F32)
        for c, column in enumerate(load_grad(grad, n)):
            wide[n, pl.ds(c, Q, stride=Q), :] = column[0:Q]
        total = total + dot(wide[n].astype(BF16), to_plain[n * TILE : (n + 1) * TILE, :])
    full[...] = total
    outs = (g0, g1, g2, g3)
    store_quarters(full, outs)
    exact = field_part[...]
    coarse = exact.astype(BF16).astype(F32)
    rest = exact - coarse
    tail = jnp.concatenate(
        [coarse[0:16], jnp.concatenate([coarse[16:24], rest[0:8]], axis=0), rest[8:24],
         jnp.zeros((16, TILE), F32)], axis=1,
    ).astype(BF16)
    for out in outs:
        out[QUARTER:TILE, :] = tail


def own_grad(keys, bounds, place, far, resid, field_part):
    return pl.pallas_call(
        own_grad_kernel,
        out_shape=(jax.ShapeDtypeStruct((TILE, PAIRS), BF16),) * 4,
        in_specs=[VMEM, SMEM] + [VMEM] * 4,
        out_specs=(VMEM,) * 4,
        scratch_shapes=[
            pltpu.VMEM((TILES, DUOS, QP, TILE), F32),
            pltpu.VMEM((WIDE, PADQ, TILE), F32),
            pltpu.VMEM((PADQ, PAIRS), F32),
            pltpu.VMEM((TILES, DEEP, SEQ), BF16),
        ],
        compiler_params=PARAMS,
        cost_estimate=pl.CostEstimate(
            flops=6_000_000_000, bytes_accessed=8_000_000, transcendentals=0
        ),
        name="own_grad",
    )(keys, bounds, place, far, resid, field_part)


def join_kernel(scale, mine, r1, r2, r3, remote, out, field_out):
    total = mine[...].astype(F32) + r1[...].astype(F32)
    total = total + (r2[...].astype(F32) + r3[...].astype(F32))
    summed = remote[0].astype(F32) + remote[1].astype(F32)
    summed = summed + (remote[2].astype(F32) + remote[3].astype(F32))
    flipped = jnp.transpose(summed)
    out[...] = ((total[0:QUARTER] + flipped[0:QUARTER]) * scale).astype(SENT)
    tail = total[QUARTER:TILE]
    first = tail[:, 0:TILE]
    middle = tail[:, TILE : 2 * TILE]
    last = tail[:, 2 * TILE : 3 * TILE]
    coarse = jnp.concatenate([first, middle[0:8]], axis=0)
    rest = jnp.concatenate([middle[8:16], last], axis=0)
    field_out[...] = ((coarse + rest) * scale)[0:Q, 0:RL]


def join_parts(scale, chunks, remote):
    return pl.pallas_call(
        functools.partial(join_kernel, scale),
        out_shape=(
            jax.ShapeDtypeStruct((QUARTER, PAIRS), SENT),
            jax.ShapeDtypeStruct((Q, RL), F32),
        ),
        in_specs=[VMEM] * 5,
        out_specs=(VMEM, VMEM),
        compiler_params=SMALL,
        name="join_parts",
    )(*chunks, remote)


def place_kernel(c0, c1, c2, c3, out, wide):
    for back, part in enumerate((c0, c1, c2, c3)):
        owner = lax.rem(lax.axis_index("seq") + (4 - back), 4)
        wide[pl.ds(pl.multiple_of(owner * QUARTER, 8), QUARTER), :] = part[...].astype(F32)
    out[...] = wide[0 : Q * Q, :]


def place_parts(chunks):
    return pl.pallas_call(
        place_kernel,
        out_shape=jax.ShapeDtypeStruct((Q * Q, PAIRS), F32),
        in_specs=[VMEM] * 4,
        out_specs=VMEM,
        scratch_shapes=[pltpu.VMEM((PADQ, PAIRS), F32)],
        compiler_params=SMALL,
        name="place_parts",
    )(*chunks)


def shifted(array, k):
    return lax.ppermute(array, "seq", [(i, (i + k) % 4) for i in range(4)])


def gather_seq(array):
    return [array] + [shifted(array, k) for k in (1, 2, 3)]


def scatter_seq(quarters):
    return [quarters[0]] + [shifted(quarters[k], k) for k in (1, 2, 3)]


def swap_blocks(array):
    blocks = array.reshape(BLOCKS, CAP, array.shape[1])
    moved = lax.all_to_all(blocks, "res", split_axis=0, concat_axis=0, tiled=True)
    return moved.reshape(array.shape)


def swap_quarters(array):
    blocks = array.reshape(4 * BLOCKS, CAP, TILE)
    moved = lax.all_to_all(blocks, ("seq", "res"), split_axis=0, concat_axis=0, tiled=True)
    return moved.reshape(4, PAIRS, TILE)


def per_device(
    alignment, seq_weights, fields, couplings, pair_left, pair_slot, slot_residue, pair_count
):
    scale = Q / (SEQ * 4)
    coup = couplings.T
    pack = pack_pairs(
        coup, pair_left[None, :], pair_slot[None, :], slot_residue[None, :], pair_count[None, :]
    )
    received = swap_blocks(pack)
    states, far, place, keys, bounds, field = own_field(alignment, pack, coup)
    remote_grad, resid, field_part = recv_half(received, states, field, fields.T, seq_weights[None, :])
    swapped = swap_quarters(remote_grad)
    local_quarters = own_grad(keys, bounds, place, far, resid, field_part)
    local_chunks = scatter_seq(local_quarters)
    joined, field_grad = join_parts(scale, local_chunks, swapped)
    coupling_grad = place_parts(gather_seq(joined))
    return coupling_grad.T, field_grad.T


def solution(mesh):
    in_specs = (
        P(None, "seq"),
        P("seq"),
        P("res", None),
        P("res", None),
        P("res"),
        P("res"),
        P("res"),
        P("res"),
    )
    out_specs = (P("res", None), P("res", None))
    return jax.shard_map(
        per_device, mesh=mesh, in_specs=in_specs, out_specs=out_specs, check_vma=False
    )
```

```python
import functools

import jax
import jax.numpy as jnp
from jax import lax
from jax.experimental import pallas as pl
from jax.experimental.pallas import tpu as pltpu
from jax.sharding import PartitionSpec as P

Q = 21
QP = 24
RL = 48
CAP = 8
SLOTS = 4
PAIRS = 512
BLOCKS = 64
SEQ = 256
RES = 3072
TILE = 128
WIDE = PAIRS // TILE
SPAN = 64
TILES = PAIRS // SPAN
DUOS = (Q + 1) // 2
ROWS = RL * QP
WINDOW = 16
WROWS = WINDOW * QP
QUARTER = 112
PADQ = 4 * QUARTER
DEEP = DUOS * TILE
F32 = jnp.float32
BF16 = jnp.bfloat16
VMEM = pl.BlockSpec(memory_space=pltpu.VMEM)
SMEM = pl.BlockSpec(memory_space=pltpu.SMEM)
PARAMS = pltpu.CompilerParams(vmem_limit_bytes=20 * 1024 * 1024)
LARGE = pltpu.CompilerParams(vmem_limit_bytes=56 * 1024 * 1024)
SMALL = pltpu.CompilerParams(vmem_limit_bytes=16 * 1024 * 1024)
SENT = BF16


def iota(shape, dim):
    return lax.broadcasted_iota(jnp.int32, shape, dim)


def dot(x, y):
    return jnp.dot(x, y, preferred_element_type=F32)


def pack_kernel(coup, left, slot, residue, count, out, wide, held, sems):
    wide[Q * Q // 8 * 8 : PADQ, :] = jnp.zeros((PADQ - Q * Q // 8 * 8, PAIRS), F32)
    wide[0 : Q * Q, :] = coup[...].astype(F32)
    lane = iota((1, PAIRS), 1)
    bucket = lax.shift_right_logical(lane, 3)
    wanted = bucket * SLOTS + slot[...]
    pick = jnp.where(iota((BLOCKS * SLOTS, PAIRS), 0) == wanted, 1.0, 0.0).astype(BF16)
    partner = dot(jnp.broadcast_to(residue[...], (8, BLOCKS * SLOTS)).astype(F32).astype(BF16), pick)
    spread = jnp.where(iota((BLOCKS, PAIRS), 0) == bucket, 1.0, 0.0).astype(BF16)
    counts = dot(jnp.broadcast_to(count[...], (8, BLOCKS)).astype(F32).astype(BF16), spread)
    live = jnp.where((lane & (CAP - 1)).astype(F32) < counts[0:1], 1.0, 0.0)
    sub = iota((16, PAIRS), 0)
    index = jnp.where(sub == 0, left[...].astype(F32), 0.0)
    index = jnp.where(sub == 1, partner[0:1], index)
    index = jnp.where(sub == 2, live, index)
    index = jnp.where(sub == 3, lax.axis_index("res").astype(F32), index)
    index = jnp.where(sub == 4, bucket.astype(F32), index)
    copies = []
    for n in range(4):
        part = jnp.concatenate([wide[n * QUARTER : (n + 1) * QUARTER, :], index], axis=0)
        held[n] = jnp.transpose(part).astype(BF16)
        lanes = slice(n * TILE, (n + 1) * TILE)
        copies.append(pltpu.make_async_copy(held.at[n], out.at[:, lanes], sems.at[n]))
        copies[n].start()
    for copy in copies:
        copy.wait()


def pack_pairs(coup, left, slot, residue, count):
    return pl.pallas_call(
        pack_kernel,
        out_shape=jax.ShapeDtypeStruct((PAIRS, 4 * TILE), BF16),
        in_specs=[VMEM] * 5,
        out_specs=pl.BlockSpec(memory_space=pl.ANY),
        scratch_shapes=[
            pltpu.VMEM((PADQ, PAIRS), F32),
            pltpu.VMEM((4, PAIRS, TILE), BF16),
            pltpu.SemaphoreType.DMA((4,)),
        ],
        compiler_params=LARGE,
        name="pack_pairs",
    )(coup, left, slot, residue, count)


def order_half(pack, flipped, own):
    mine, other, block = (112, 113, 116) if own else (113, 112, 115)
    wide = pack.astype(F32)
    key_row = jnp.where(flipped[114:115] > 0.5, flipped[mine : mine + 1], float(RL))
    key_col = jnp.where(wide[:, 114:115] > 0.5, wide[:, mine : mine + 1], float(RL))
    lane = iota((PAIRS, PAIRS), 1).astype(F32)
    sub = iota((PAIRS, PAIRS), 0).astype(F32)
    full_row = key_row * PAIRS + lane
    full_col = key_col * PAIRS + sub
    place_row = jnp.sum(jnp.where(full_col < full_row, 1.0, 0.0), axis=0, keepdims=True)
    place_col = jnp.sum(jnp.where(full_row < full_col, 1.0, 0.0), axis=1, keepdims=True)
    to_sorted = jnp.where(place_col == lane, 1.0, 0.0).astype(BF16)
    to_plain = jnp.where(place_row == sub, 1.0, 0.0).astype(BF16)
    far = wide[:, block : block + 1] * RL + wide[:, other : other + 1]
    keys = dot(jnp.broadcast_to(key_row, (8, PAIRS)).astype(BF16), to_sorted)
    return to_sorted, to_plain, place_row, far, keys


def plain_order(place):
    return jnp.where(place[0:1] == iota((PAIRS, PAIRS), 0).astype(F32), 1.0, 0.0).astype(BF16)


def find_far(far, states, to_plain, plain):
    count = 4
    for start in range(0, BLOCKS, count):
        blocks = min(count, BLOCKS - start)
        pairs = slice(start * CAP, (start + blocks) * CAP)
        base = start * RL
        depth = min(256, RES - base)
        lane = iota((blocks * CAP, depth), 1).astype(F32)
        pick = jnp.where(far[pairs] - float(base) == lane, 1.0, 0.0).astype(BF16)
        plain[pairs, :] = dot(pick, states[base : base + depth, :].astype(BF16))
    return dot(to_plain, plain[...].astype(BF16))


def fill_hot(far, j, hot):
    tile = far[pl.ds(pl.multiple_of(j * SPAN, SPAN), SPAN), :].astype(F32)
    for c in range(2 * DUOS):
        hot[j, c * SPAN : (c + 1) * SPAN, :] = jnp.where(tile == float(c), 1.0, 0.0).astype(BF16)


def halves(first, second):
    low = iota(first.shape, 1) < SPAN
    return (
        jnp.where(low, first, pltpu.roll(second, SPAN, 1)),
        jnp.where(low, pltpu.roll(first, SPAN, 1), second),
    )


def store_keys(keys, keys_ref, bounds):
    for n in range(WIDE):
        part = keys[:, n * TILE : (n + 1) * TILE]
        for i, span in enumerate(halves(part, part)):
            j = 2 * n + i
            keys_ref[j] = span
            bounds[0, j], bounds[1, j] = window_range(span)


def store_blocks(block, n, blocks):
    for d in range(DUOS):
        second = block(2 * d + 1) if 2 * d + 1 < Q else jnp.zeros((QP, TILE), F32)
        blocks[2 * n, d], blocks[2 * n + 1, d] = halves(block(2 * d), second)


def load_grad(grad, n):
    columns = []
    for d in range(DUOS):
        columns.extend(halves(grad[2 * n, d], grad[2 * n + 1, d]))
    return columns[:Q]


def window_range(keys):
    low = jnp.min(keys).astype(jnp.int32)
    high = jnp.max(jnp.where(keys < RL - 0.5, keys, -1.0)).astype(jnp.int32)
    first = low - (low & 1)
    return first, jnp.where(high >= 0, (high - first) // WINDOW + 1, 0)


def window_at(keys, first, step):
    start = first + step * WINDOW
    base = jnp.minimum(start, RL - WINDOW)
    fresh = jnp.where(keys[0:1] >= start.astype(F32), keys[0:1], -1.0)
    wide = jnp.broadcast_to(fresh, (QP, TILE))
    rows = pl.ds(pl.multiple_of(base * QP, 2 * QP), WROWS)
    return rows, [wide == (base + m).astype(F32) for m in range(WINDOW)]


def add_field(keys_ref, bounds, blocks, far, hot, lhs, field):
    def tile_step(j, carry):
        keys = keys_ref[j]
        first, count = bounds[0, j], bounds[1, j]

        @pl.when(count > 0)
        def _():
            fill_hot(far, j, hot)

        def window_step(step, carry):
            window, masks = window_at(keys, first, step)
            for d in range(DUOS):
                block = blocks[j, d]
                rows = [jnp.where(mask, block, 0.0) for mask in masks]
                lhs[:, d * TILE : (d + 1) * TILE] = jnp.concatenate(rows, axis=0).astype(BF16)
            field[window, :] += dot(lhs[...], hot[j])
            return carry

        return lax.fori_loop(0, count, window_step, carry)

    lax.fori_loop(0, TILES, tile_step, 0)


def add_grad(keys_ref, bounds, resid, hot, grad, far=None):
    grad[...] = jnp.zeros_like(grad)

    def tile_step(j, carry):
        keys = keys_ref[j]
        first, count = bounds[0, j], bounds[1, j]
        if far is not None:

            @pl.when(count > 0)
            def _():
                fill_hot(far, j, hot)

        def window_step(step, carry):
            window, masks = window_at(keys, first, step)
            rows = resid[window, :]
            for d in range(0, DUOS, 2):
                duos = min(2, DUOS - d)
                part = hot[j, d * TILE : (d + duos) * TILE, :]
                out = lax.dot_general(
                    rows, part, (((1,), (1,)), ((), ())), preferred_element_type=F32
                )
                for i in range(duos):
                    total = grad[j, d + i]
                    for m in range(WINDOW):
                        piece = out[m * QP : (m + 1) * QP, i * TILE : (i + 1) * TILE]
                        total = jnp.where(masks[m], piece, total)
                    grad[j, d + i] = total
            return carry

        return lax.fori_loop(0, count, window_step, carry)

    lax.fori_loop(0, TILES, tile_step, 0)


def store_quarters(full, outs):
    seq_index = lax.axis_index("seq")
    for k, out in enumerate(outs):
        owner = lax.rem(seq_index + k, 4)
        out[0:QUARTER, :] = full[pl.ds(pl.multiple_of(owner * QUARTER, 8), QUARTER), :].astype(BF16)


def own_field_kernel(
    alignment, pack, coup, states_out, codes_out, far_out, place_out, keys_ref, bounds, field,
    sorted_blocks, blocks, hot, lhs, codes, plain, states,
):
    chunk = 512
    parts = [slice(n * chunk, (n + 1) * chunk) for n in range(RES // chunk)]
    packed = pack[:, 0:TILE]
    flipped = jnp.transpose(packed.astype(F32))
    to_sorted, to_plain, place, far, keys = order_half(packed, flipped, True)
    place_out[...] = jnp.broadcast_to(place, (8, PAIRS))
    store_keys(keys, keys_ref, bounds)
    sorted_blocks[...] = jnp.zeros_like(sorted_blocks)
    ordered = dot(coup[...], to_sorted)
    for n in range(WIDE):
        sorted_blocks[n, 0 : Q * Q, :] = ordered[:, n * TILE : (n + 1) * TILE]
        store_blocks(lambda c: sorted_blocks[n, pl.ds(c, QP, stride=Q), :], n, blocks)
    field[...] = jnp.zeros_like(field)
    for rows in parts:
        part = alignment[rows, :]
        states[rows, :] = part.astype(F32).astype(BF16)
        states_out[rows, :] = part.astype(jnp.int8)
    mine = pl.ds(pl.multiple_of(lax.axis_index("res") * RL, 16), RL)
    codes_out[...] = states[mine, :]
    far_states = find_far(far, states, to_plain, plain)
    far_out[...] = far_states.astype(jnp.int8)
    codes[...] = far_states.astype(BF16)
    add_field(keys_ref, bounds, blocks, codes, hot, lhs, field)


def own_field(alignment, pack, coup):
    return pl.pallas_call(
        own_field_kernel,
        out_shape=(
            jax.ShapeDtypeStruct((RES, SEQ), jnp.int8),
            jax.ShapeDtypeStruct((RL, SEQ), BF16),
            jax.ShapeDtypeStruct((PAIRS, SEQ), jnp.int8),
            jax.ShapeDtypeStruct((8, PAIRS), F32),
            jax.ShapeDtypeStruct((TILES, 8, TILE), F32),
            jax.ShapeDtypeStruct((2, TILES), jnp.int32),
            jax.ShapeDtypeStruct((ROWS, SEQ), F32),
        ),
        in_specs=[VMEM, VMEM, VMEM],
        out_specs=(VMEM,) * 5 + (SMEM, VMEM),
        scratch_shapes=[
            pltpu.VMEM((WIDE, 512, TILE), F32),
            pltpu.VMEM((TILES, DUOS, QP, TILE), F32),
            pltpu.VMEM((TILES, DEEP, SEQ), BF16),
            pltpu.VMEM((WROWS, DEEP), BF16),
            pltpu.VMEM((PAIRS, SEQ), BF16),
            pltpu.VMEM((PAIRS, SEQ), F32),
            pltpu.VMEM((RES, SEQ), BF16),
        ],
        compiler_params=PARAMS,
        cost_estimate=pl.CostEstimate(
            flops=10_000_000_000, bytes_accessed=10_000_000, transcendentals=0
        ),
        name="own_field",
    )(alignment, pack, coup)


def recv_kernel(
    parts, states, codes, own, fields, weights,
    grad_out, resid_out, field_out,
    wide, sorted_blocks, blocks, hot, lhs, field, grad, far, plain, keys_ref, bounds,
):
    packed = parts[:, 0:TILE]
    flipped = jnp.transpose(packed.astype(F32))
    to_sorted, to_plain, place, far_col, keys = order_half(packed, flipped, False)
    store_keys(keys, keys_ref, bounds)
    far[...] = find_far(far_col, states, to_plain, plain).astype(BF16)
    for n in range(4):
        if n > 0:
            flipped = jnp.transpose(parts[:, n * TILE : (n + 1) * TILE].astype(F32))
        wide[n * QUARTER : (n + 1) * QUARTER, :] = flipped[0:QUARTER]
    sorted_blocks[PADQ:512, :] = jnp.zeros((512 - PADQ, PAIRS), F32)
    sorted_blocks[0:PADQ, :] = dot(wide[0:PADQ, :].astype(BF16), to_sorted)
    for n in range(WIDE):
        lanes = slice(n * TILE, (n + 1) * TILE)
        store_blocks(lambda a: sorted_blocks[a * Q : a * Q + QP, lanes], n, blocks)
    field[...] = own[...]
    add_field(keys_ref, bounds, blocks, far, hot, lhs, field)

    my_codes = codes[...].astype(F32)
    state = iota((QP, SEQ), 0).astype(F32)
    weight = weights[...]
    lane = iota((QP, TILE), 1)
    local = jnp.concatenate([fields[...], jnp.full((QP - Q, RL), -1e30, F32)], axis=0)
    field_part = jnp.zeros((QP, TILE), F32)
    ones = jnp.ones((SEQ, TILE), BF16)
    for r in range(0, RL, 2):
        pieces = []
        for m in (r, r + 1):
            logits = field[m * QP : (m + 1) * QP, :] + local[:, m : m + 1]
            top = jnp.max(logits, axis=0, keepdims=True)
            raised = jnp.exp(logits - top)
            share = weight / jnp.sum(raised, axis=0, keepdims=True)
            hot_own = jnp.where(state == my_codes[m : m + 1], weight, 0.0)
            pieces.append(raised * share - hot_own)
        resid_out[r * QP : (r + 2) * QP, :] = jnp.concatenate(pieces, axis=0).astype(BF16)
    sums = dot(resid_out[...], ones)
    for r in range(RL):
        field_part = jnp.where(lane == r, sums[r * QP : (r + 1) * QP], field_part)
    field_out[...] = field_part

    add_grad(keys_ref, bounds, resid_out, hot, grad)
    for n in range(4):
        wide[n * TILE + QUARTER : (n + 1) * TILE, :] = jnp.zeros((TILE - QUARTER, PAIRS), F32)
    last = 3 * TILE + Q * Q - 3 * QUARTER
    wide[last // 8 * 8 : 3 * TILE + QUARTER, :] = jnp.zeros((3 * TILE + QUARTER - last // 8 * 8, PAIRS), F32)
    for n in range(WIDE):
        lanes = slice(n * TILE, (n + 1) * TILE)
        for a, column in enumerate(load_grad(grad, n)):
            done = 0
            while done < Q:
                quarter, row = divmod(a * Q + done, QUARTER)
                size = min(Q - done, QUARTER - row)
                start = quarter * TILE + row
                wide[start : start + size, lanes] = column[done : done + size]
                done += size
    result = lax.dot_general(
        to_sorted, wide[...].astype(BF16), (((1,), (1,)), ((), ())), preferred_element_type=F32
    )
    for n in range(4):
        grad_out[n] = result[:, n * TILE : (n + 1) * TILE].astype(BF16)


def recv_half(received, states, codes, own, fields, weights):
    return pl.pallas_call(
        recv_kernel,
        out_shape=(
            jax.ShapeDtypeStruct((4, PAIRS, TILE), BF16),
            jax.ShapeDtypeStruct((ROWS, SEQ), BF16),
            jax.ShapeDtypeStruct((QP, TILE), F32),
        ),
        in_specs=[VMEM] * 6,
        out_specs=(VMEM,) * 3,
        scratch_shapes=[
            pltpu.VMEM((4 * TILE, PAIRS), F32),
            pltpu.VMEM((512, PAIRS), F32),
            pltpu.VMEM((TILES, DUOS, QP, TILE), F32),
            pltpu.VMEM((TILES, DEEP, SEQ), BF16),
            pltpu.VMEM((WROWS, DEEP), BF16),
            pltpu.VMEM((ROWS, SEQ), F32),
            pltpu.VMEM((TILES, DUOS, QP, TILE), F32),
            pltpu.VMEM((PAIRS, SEQ), BF16),
            pltpu.VMEM((PAIRS, SEQ), F32),
            pltpu.VMEM((TILES, 8, TILE), F32),
            pltpu.SMEM((2, TILES), jnp.int32),
        ],
        compiler_params=PARAMS,
        cost_estimate=pl.CostEstimate(
            flops=20_000_000_000, bytes_accessed=10_000_000, transcendentals=0
        ),
        name="recv_half",
    )(received, states, codes, own, fields, weights)


def own_grad_kernel(
    keys_ref, bounds, place, far, resid, field_part, g0, g1, g2, g3, grad, wide, full, hot, rows
):
    add_grad(keys_ref, bounds, resid, hot, grad, far)
    for n in range(WIDE):
        wide[n, Q * Q // 8 * 8 : PADQ, :] = jnp.zeros((PADQ - Q * Q // 8 * 8, TILE), F32)
        for c, column in enumerate(load_grad(grad, n)):
            wide[n, pl.ds(c, Q, stride=Q), :] = column[0:Q]
        rows[:, n * TILE : (n + 1) * TILE] = wide[n].astype(BF16)
    full[...] = dot(rows[...], plain_order(place))
    outs = (g0, g1, g2, g3)
    store_quarters(full, outs)
    exact = field_part[...]
    coarse = exact.astype(BF16).astype(F32)
    rest = exact - coarse
    tail = jnp.concatenate(
        [coarse[0:16], jnp.concatenate([coarse[16:24], rest[0:8]], axis=0), rest[8:24],
         jnp.zeros((16, TILE), F32)], axis=1,
    ).astype(BF16)
    for out in outs:
        out[QUARTER:TILE, :] = tail


def own_grad(keys, bounds, place, far, resid, field_part):
    return pl.pallas_call(
        own_grad_kernel,
        out_shape=(jax.ShapeDtypeStruct((TILE, PAIRS), BF16),) * 4,
        in_specs=[VMEM, SMEM] + [VMEM] * 4,
        out_specs=(VMEM,) * 4,
        scratch_shapes=[
            pltpu.VMEM((TILES, DUOS, QP, TILE), F32),
            pltpu.VMEM((WIDE, PADQ, TILE), F32),
            pltpu.VMEM((PADQ, PAIRS), F32),
            pltpu.VMEM((TILES, DEEP, SEQ), BF16),
            pltpu.VMEM((PADQ, PAIRS), BF16),
        ],
        compiler_params=PARAMS,
        cost_estimate=pl.CostEstimate(
            flops=6_000_000_000, bytes_accessed=8_000_000, transcendentals=0
        ),
        name="own_grad",
    )(keys, bounds, place, far, resid, field_part)


def join_kernel(scale, mine, r1, r2, r3, remote, out, field_out):
    total = mine[...].astype(F32) + r1[...].astype(F32)
    total = total + (r2[...].astype(F32) + r3[...].astype(F32))
    summed = remote[0].astype(F32) + remote[1].astype(F32)
    summed = summed + (remote[2].astype(F32) + remote[3].astype(F32))
    flipped = jnp.transpose(summed)
    out[...] = ((total[0:QUARTER] + flipped[0:QUARTER]) * scale).astype(SENT)
    tail = total[QUARTER:TILE]
    first = tail[:, 0:TILE]
    middle = tail[:, TILE : 2 * TILE]
    last = tail[:, 2 * TILE : 3 * TILE]
    coarse = jnp.concatenate([first, middle[0:8]], axis=0)
    rest = jnp.concatenate([middle[8:16], last], axis=0)
    field_out[...] = ((coarse + rest) * scale)[0:Q, 0:RL]


def join_parts(scale, chunks, remote):
    return pl.pallas_call(
        functools.partial(join_kernel, scale),
        out_shape=(
            jax.ShapeDtypeStruct((QUARTER, PAIRS), SENT),
            jax.ShapeDtypeStruct((Q, RL), F32),
        ),
        in_specs=[VMEM] * 5,
        out_specs=(VMEM, VMEM),
        compiler_params=SMALL,
        name="join_parts",
    )(*chunks, remote)


def place_kernel(c0, c1, c2, c3, out):
    short = Q * Q - 3 * QUARTER
    for back, part in enumerate((c0, c1, c2, c3)):
        owner = lax.rem(lax.axis_index("seq") + (4 - back), 4)

        @pl.when(owner < 3)
        def _():
            out[pl.ds(pl.multiple_of(owner * QUARTER, 8), QUARTER), :] = part[...].astype(F32)

        @pl.when(owner == 3)
        def _():
            out[3 * QUARTER : Q * Q, :] = part[0:short, :].astype(F32)


def place_parts(chunks):
    return pl.pallas_call(
        place_kernel,
        out_shape=jax.ShapeDtypeStruct((Q * Q, PAIRS), F32),
        in_specs=[VMEM] * 4,
        out_specs=VMEM,
        compiler_params=SMALL,
        name="place_parts",
    )(*chunks)


def shifted(array, k):
    return lax.ppermute(array, "seq", [(i, (i + k) % 4) for i in range(4)])


def gather_seq(array):
    return [array] + [shifted(array, k) for k in (1, 2, 3)]


def scatter_seq(quarters):
    return [quarters[0]] + [shifted(quarters[k], k) for k in (1, 2, 3)]


def swap_blocks(array):
    blocks = array.reshape(BLOCKS, CAP, array.shape[1])
    moved = lax.all_to_all(blocks, "res", split_axis=0, concat_axis=0, tiled=True)
    return moved.reshape(array.shape)


def swap_quarters(array):
    blocks = array.reshape(4 * BLOCKS, CAP, TILE)
    moved = lax.all_to_all(blocks, ("seq", "res"), split_axis=0, concat_axis=0, tiled=True)
    return moved.reshape(4, PAIRS, TILE)


def per_device(
    alignment, seq_weights, fields, couplings, pair_left, pair_slot, slot_residue, pair_count
):
    scale = Q / (SEQ * 4)
    coup = couplings.T
    pack = pack_pairs(
        coup, pair_left[None, :], pair_slot[None, :], slot_residue[None, :], pair_count[None, :]
    )
    received = swap_blocks(pack)
    states, codes, far, place, keys, bounds, field = own_field(alignment, pack, coup)
    remote_grad, resid, field_part = recv_half(received, states, codes, field, fields.T, seq_weights[None, :])
    swapped = swap_quarters(remote_grad)
    local_quarters = own_grad(keys, bounds, place, far, resid, field_part)
    local_chunks = scatter_seq(local_quarters)
    joined, field_grad = join_parts(scale, local_chunks, swapped)
    coupling_grad = place_parts(gather_seq(joined))
    return coupling_grad.T, field_grad.T


def solution(mesh):
    in_specs = (
        P(None, "seq"),
        P("seq"),
        P("res", None),
        P("res", None),
        P("res"),
        P("res"),
        P("res"),
        P("res"),
    )
    out_specs = (P("res", None), P("res", None))
    return jax.shard_map(
        per_device, mesh=mesh, in_specs=in_specs, out_specs=out_specs, check_vma=False
    )
```

```python
import functools

import jax
import jax.numpy as jnp
from jax import lax
from jax.experimental import pallas as pl
from jax.experimental.pallas import tpu as pltpu
from jax.sharding import PartitionSpec as P

Q = 21
QP = 24
RL = 48
CAP = 8
SLOTS = 4
PAIRS = 512
BLOCKS = 64
SEQ = 256
RES = 3072
TILE = 128
WIDE = PAIRS // TILE
SPAN = 64
TILES = PAIRS // SPAN
DUOS = (Q + 1) // 2
ROWS = RL * QP
WINDOW = 16
WROWS = WINDOW * QP
QUARTER = 112
PADQ = 4 * QUARTER
DEEP = DUOS * TILE
F32 = jnp.float32
BF16 = jnp.bfloat16
VMEM = pl.BlockSpec(memory_space=pltpu.VMEM)
SMEM = pl.BlockSpec(memory_space=pltpu.SMEM)
PARAMS = pltpu.CompilerParams(vmem_limit_bytes=20 * 1024 * 1024)
LARGE = pltpu.CompilerParams(vmem_limit_bytes=56 * 1024 * 1024)
SMALL = pltpu.CompilerParams(vmem_limit_bytes=16 * 1024 * 1024)
SENT = BF16


def iota(shape, dim):
    return lax.broadcasted_iota(jnp.int32, shape, dim)


def dot(x, y):
    return jnp.dot(x, y, preferred_element_type=F32)


def pack_kernel(coup, left, slot, residue, count, out, wide, held, sems):
    wide[Q * Q // 8 * 8 : PADQ, :] = jnp.zeros((PADQ - Q * Q // 8 * 8, PAIRS), F32)
    wide[0 : Q * Q, :] = coup[...].astype(F32)
    lane = iota((1, PAIRS), 1)
    bucket = lax.shift_right_logical(lane, 3)
    wanted = bucket * SLOTS + slot[...]
    pick = jnp.where(iota((BLOCKS * SLOTS, PAIRS), 0) == wanted, 1.0, 0.0).astype(BF16)
    partner = dot(jnp.broadcast_to(residue[...], (8, BLOCKS * SLOTS)).astype(F32).astype(BF16), pick)
    spread = jnp.where(iota((BLOCKS, PAIRS), 0) == bucket, 1.0, 0.0).astype(BF16)
    counts = dot(jnp.broadcast_to(count[...], (8, BLOCKS)).astype(F32).astype(BF16), spread)
    live = jnp.where((lane & (CAP - 1)).astype(F32) < counts[0:1], 1.0, 0.0)
    sub = iota((16, PAIRS), 0)
    index = jnp.where(sub == 0, left[...].astype(F32), 0.0)
    index = jnp.where(sub == 1, partner[0:1], index)
    index = jnp.where(sub == 2, live, index)
    index = jnp.where(sub == 3, lax.axis_index("res").astype(F32), index)
    index = jnp.where(sub == 4, bucket.astype(F32), index)
    copies = []
    for n in range(4):
        part = jnp.concatenate([wide[n * QUARTER : (n + 1) * QUARTER, :], index], axis=0)
        held[n] = jnp.transpose(part).astype(BF16)
        lanes = slice(n * TILE, (n + 1) * TILE)
        copies.append(pltpu.make_async_copy(held.at[n], out.at[:, lanes], sems.at[n]))
        copies[n].start()
    for copy in copies:
        copy.wait()


def pack_pairs(coup, left, slot, residue, count):
    return pl.pallas_call(
        pack_kernel,
        out_shape=jax.ShapeDtypeStruct((PAIRS, 4 * TILE), BF16),
        in_specs=[VMEM] * 5,
        out_specs=pl.BlockSpec(memory_space=pl.ANY),
        scratch_shapes=[
            pltpu.VMEM((PADQ, PAIRS), F32),
            pltpu.VMEM((4, PAIRS, TILE), BF16),
            pltpu.SemaphoreType.DMA((4,)),
        ],
        compiler_params=LARGE,
        name="pack_pairs",
    )(coup, left, slot, residue, count)


def order_half(pack, flipped, own):
    mine, other, block = (112, 113, 116) if own else (113, 112, 115)
    wide = pack.astype(F32)
    key_row = jnp.where(flipped[114:115] > 0.5, flipped[mine : mine + 1], float(RL))
    key_col = jnp.where(wide[:, 114:115] > 0.5, wide[:, mine : mine + 1], float(RL))
    lane = iota((PAIRS, PAIRS), 1).astype(F32)
    sub = iota((PAIRS, PAIRS), 0).astype(F32)
    full_row = key_row * PAIRS + lane
    full_col = key_col * PAIRS + sub
    place_row = jnp.sum(jnp.where(full_col < full_row, 1.0, 0.0), axis=0, keepdims=True)
    place_col = jnp.sum(jnp.where(full_row < full_col, 1.0, 0.0), axis=1, keepdims=True)
    to_sorted = jnp.where(place_col == lane, 1.0, 0.0).astype(BF16)
    to_plain = jnp.where(place_row == sub, 1.0, 0.0).astype(BF16)
    far = wide[:, block : block + 1] * RL + wide[:, other : other + 1]
    keys = dot(jnp.broadcast_to(key_row, (8, PAIRS)).astype(BF16), to_sorted)
    return to_sorted, to_plain, place_row, far, keys


def plain_order(place):
    return jnp.where(place[0:1] == iota((PAIRS, PAIRS), 0).astype(F32), 1.0, 0.0).astype(BF16)


def find_far(far, states, to_plain, plain):
    count = 4
    for start in range(0, BLOCKS, count):
        blocks = min(count, BLOCKS - start)
        pairs = slice(start * CAP, (start + blocks) * CAP)
        base = start * RL
        depth = min(256, RES - base)
        lane = iota((blocks * CAP, depth), 1).astype(F32)
        pick = jnp.where(far[pairs] - float(base) == lane, 1.0, 0.0).astype(BF16)
        plain[pairs, :] = dot(pick, states[base : base + depth, :].astype(BF16))
    return dot(to_plain, plain[...].astype(BF16))


def fill_hot(far, j, hot):
    tile = far[pl.ds(pl.multiple_of(j * SPAN, SPAN), SPAN), :].astype(BF16)
    one, none = jnp.ones_like(tile), jnp.zeros_like(tile)
    for c in range(2 * DUOS):
        hot[j, c * SPAN : (c + 1) * SPAN, :] = jnp.where(tile == jnp.array(c, BF16), one, none)


def halves(first, second):
    low = iota(first.shape, 1) < SPAN
    return (
        jnp.where(low, first, pltpu.roll(second, SPAN, 1)),
        jnp.where(low, pltpu.roll(first, SPAN, 1), second),
    )


def store_keys(keys, keys_ref, bounds):
    for n in range(WIDE):
        part = keys[:, n * TILE : (n + 1) * TILE]
        for i, span in enumerate(halves(part, part)):
            j = 2 * n + i
            keys_ref[j] = span
            bounds[0, j], bounds[1, j] = window_range(span)


def store_blocks(block, n, blocks):
    for d in range(DUOS):
        second = block(2 * d + 1) if 2 * d + 1 < Q else jnp.zeros((QP, TILE), F32)
        blocks[2 * n, d], blocks[2 * n + 1, d] = halves(block(2 * d), second)


def load_grad(grad, n):
    columns = []
    for d in range(DUOS):
        columns.extend(halves(grad[2 * n, d], grad[2 * n + 1, d]))
    return columns[:Q]


def window_range(keys):
    low = jnp.min(keys).astype(jnp.int32)
    high = jnp.max(jnp.where(keys < RL - 0.5, keys, -1.0)).astype(jnp.int32)
    first = low - (low & 1)
    return first, jnp.where(high >= 0, (high - first) // WINDOW + 1, 0)


def window_at(keys, first, step):
    start = first + step * WINDOW
    base = jnp.minimum(start, RL - WINDOW)
    fresh = jnp.where(keys[0:1] >= start.astype(F32), keys[0:1], -1.0)
    wide = jnp.broadcast_to(fresh, (QP, TILE))
    rows = pl.ds(pl.multiple_of(base * QP, 2 * QP), WROWS)
    return rows, [wide == (base + m).astype(F32) for m in range(WINDOW)]


def add_field(keys_ref, bounds, blocks, far, hot, lhs, field):
    def tile_step(j, carry):
        keys = keys_ref[j]
        first, count = bounds[0, j], bounds[1, j]

        @pl.when(count > 0)
        def _():
            fill_hot(far, j, hot)

        def window_step(step, carry):
            window, masks = window_at(keys, first, step)
            for d in range(DUOS):
                block = blocks[j, d]
                rows = [jnp.where(mask, block, 0.0) for mask in masks]
                lhs[:, d * TILE : (d + 1) * TILE] = jnp.concatenate(rows, axis=0).astype(BF16)
            field[window, :] += dot(lhs[...], hot[j])
            return carry

        return lax.fori_loop(0, count, window_step, carry)

    lax.fori_loop(0, TILES, tile_step, 0)


def add_grad(keys_ref, bounds, resid, hot, grad, far=None):
    grad[...] = jnp.zeros_like(grad)

    def tile_step(j, carry):
        keys = keys_ref[j]
        first, count = bounds[0, j], bounds[1, j]
        if far is not None:

            @pl.when(count > 0)
            def _():
                fill_hot(far, j, hot)

        def window_step(step, carry):
            window, masks = window_at(keys, first, step)
            rows = resid[window, :]
            for d in range(0, DUOS, 2):
                duos = min(2, DUOS - d)
                part = hot[j, d * TILE : (d + duos) * TILE, :]
                out = lax.dot_general(
                    rows, part, (((1,), (1,)), ((), ())), preferred_element_type=F32
                )
                for i in range(duos):
                    total = grad[j, d + i]
                    for m in range(WINDOW):
                        piece = out[m * QP : (m + 1) * QP, i * TILE : (i + 1) * TILE]
                        total = jnp.where(masks[m], piece, total)
                    grad[j, d + i] = total
            return carry

        return lax.fori_loop(0, count, window_step, carry)

    lax.fori_loop(0, TILES, tile_step, 0)


def store_quarters(full, outs):
    seq_index = lax.axis_index("seq")
    for k, out in enumerate(outs):
        owner = lax.rem(seq_index + k, 4)
        out[0:QUARTER, :] = full[pl.ds(pl.multiple_of(owner * QUARTER, 8), QUARTER), :].astype(BF16)


def own_field_kernel(
    alignment, pack, coup, states_out, codes_out, far_out, place_out, keys_ref, bounds, field,
    sorted_blocks, blocks, hot, lhs, codes, plain, states,
):
    chunk = 512
    parts = [slice(n * chunk, (n + 1) * chunk) for n in range(RES // chunk)]
    packed = pack[:, 0:TILE]
    flipped = jnp.transpose(packed.astype(F32))
    to_sorted, to_plain, place, far, keys = order_half(packed, flipped, True)
    place_out[...] = jnp.broadcast_to(place, (8, PAIRS))
    store_keys(keys, keys_ref, bounds)
    sorted_blocks[...] = jnp.zeros_like(sorted_blocks)
    ordered = dot(coup[...], to_sorted)
    for n in range(WIDE):
        sorted_blocks[n, 0 : Q * Q, :] = ordered[:, n * TILE : (n + 1) * TILE]
        store_blocks(lambda c: sorted_blocks[n, pl.ds(c, QP, stride=Q), :], n, blocks)
    field[...] = jnp.zeros_like(field)
    for rows in parts:
        part = alignment[rows, :]
        states[rows, :] = part.astype(F32).astype(BF16)
        states_out[rows, :] = part.astype(jnp.int8)
    mine = pl.ds(pl.multiple_of(lax.axis_index("res") * RL, 16), RL)
    codes_out[...] = states[mine, :]
    far_states = find_far(far, states, to_plain, plain)
    far_out[...] = far_states.astype(jnp.int8)
    codes[...] = far_states.astype(BF16)
    add_field(keys_ref, bounds, blocks, codes, hot, lhs, field)


def own_field(alignment, pack, coup):
    return pl.pallas_call(
        own_field_kernel,
        out_shape=(
            jax.ShapeDtypeStruct((RES, SEQ), jnp.int8),
            jax.ShapeDtypeStruct((RL, SEQ), BF16),
            jax.ShapeDtypeStruct((PAIRS, SEQ), jnp.int8),
            jax.ShapeDtypeStruct((8, PAIRS), F32),
            jax.ShapeDtypeStruct((TILES, 8, TILE), F32),
            jax.ShapeDtypeStruct((2, TILES), jnp.int32),
            jax.ShapeDtypeStruct((ROWS, SEQ), F32),
        ),
        in_specs=[VMEM, VMEM, VMEM],
        out_specs=(VMEM,) * 5 + (SMEM, VMEM),
        scratch_shapes=[
            pltpu.VMEM((WIDE, 512, TILE), F32),
            pltpu.VMEM((TILES, DUOS, QP, TILE), F32),
            pltpu.VMEM((TILES, DEEP, SEQ), BF16),
            pltpu.VMEM((WROWS, DEEP), BF16),
            pltpu.VMEM((PAIRS, SEQ), BF16),
            pltpu.VMEM((PAIRS, SEQ), F32),
            pltpu.VMEM((RES, SEQ), BF16),
        ],
        compiler_params=PARAMS,
        cost_estimate=pl.CostEstimate(
            flops=10_000_000_000, bytes_accessed=10_000_000, transcendentals=0
        ),
        name="own_field",
    )(alignment, pack, coup)


def recv_kernel(
    parts, states, codes, own, fields, weights,
    grad_out, resid_out, field_out,
    wide, sorted_blocks, blocks, hot, lhs, field, grad, far, plain, keys_ref, bounds,
):
    packed = parts[:, 0:TILE]
    flipped = jnp.transpose(packed.astype(F32))
    to_sorted, to_plain, place, far_col, keys = order_half(packed, flipped, False)
    store_keys(keys, keys_ref, bounds)
    far[...] = find_far(far_col, states, to_plain, plain).astype(BF16)
    for n in range(4):
        if n > 0:
            flipped = jnp.transpose(parts[:, n * TILE : (n + 1) * TILE].astype(F32))
        wide[n * QUARTER : (n + 1) * QUARTER, :] = flipped[0:QUARTER]
    sorted_blocks[PADQ:512, :] = jnp.zeros((512 - PADQ, PAIRS), F32)
    sorted_blocks[0:PADQ, :] = dot(wide[0:PADQ, :].astype(BF16), to_sorted)
    for n in range(WIDE):
        lanes = slice(n * TILE, (n + 1) * TILE)
        store_blocks(lambda a: sorted_blocks[a * Q : a * Q + QP, lanes], n, blocks)
    field[...] = own[...]
    add_field(keys_ref, bounds, blocks, far, hot, lhs, field)

    my_codes = codes[...].astype(F32)
    state = iota((QP, SEQ), 0).astype(F32)
    weight = weights[...]
    lane = iota((QP, TILE), 1)
    local = jnp.concatenate([fields[...], jnp.full((QP - Q, RL), -1e30, F32)], axis=0)
    field_part = jnp.zeros((QP, TILE), F32)
    ones = jnp.ones((SEQ, TILE), BF16)
    for r in range(0, RL, 2):
        pieces = []
        for m in (r, r + 1):
            logits = field[m * QP : (m + 1) * QP, :] + local[:, m : m + 1]
            top = jnp.max(logits, axis=0, keepdims=True)
            raised = jnp.exp(logits - top)
            share = weight / jnp.sum(raised, axis=0, keepdims=True)
            hot_own = jnp.where(state == my_codes[m : m + 1], weight, 0.0)
            pieces.append(raised * share - hot_own)
        resid_out[r * QP : (r + 2) * QP, :] = jnp.concatenate(pieces, axis=0).astype(BF16)
    sums = dot(resid_out[...], ones)
    for r in range(RL):
        field_part = jnp.where(lane == r, sums[r * QP : (r + 1) * QP], field_part)
    field_out[...] = field_part

    add_grad(keys_ref, bounds, resid_out, hot, grad)
    for n in range(4):
        wide[n * TILE + QUARTER : (n + 1) * TILE, :] = jnp.zeros((TILE - QUARTER, PAIRS), F32)
    last = 3 * TILE + Q * Q - 3 * QUARTER
    wide[last // 8 * 8 : 3 * TILE + QUARTER, :] = jnp.zeros((3 * TILE + QUARTER - last // 8 * 8, PAIRS), F32)
    for n in range(WIDE):
        lanes = slice(n * TILE, (n + 1) * TILE)
        for a, column in enumerate(load_grad(grad, n)):
            done = 0
            while done < Q:
                quarter, row = divmod(a * Q + done, QUARTER)
                size = min(Q - done, QUARTER - row)
                start = quarter * TILE + row
                wide[start : start + size, lanes] = column[done : done + size]
                done += size
    result = lax.dot_general(
        to_sorted, wide[...].astype(BF16), (((1,), (1,)), ((), ())), preferred_element_type=F32
    )
    for n in range(4):
        grad_out[n] = result[:, n * TILE : (n + 1) * TILE].astype(BF16)


def recv_half(received, states, codes, own, fields, weights):
    return pl.pallas_call(
        recv_kernel,
        out_shape=(
            jax.ShapeDtypeStruct((4, PAIRS, TILE), BF16),
            jax.ShapeDtypeStruct((ROWS, SEQ), BF16),
            jax.ShapeDtypeStruct((QP, TILE), F32),
        ),
        in_specs=[VMEM] * 6,
        out_specs=(VMEM,) * 3,
        scratch_shapes=[
            pltpu.VMEM((4 * TILE, PAIRS), F32),
            pltpu.VMEM((512, PAIRS), F32),
            pltpu.VMEM((TILES, DUOS, QP, TILE), F32),
            pltpu.VMEM((TILES, DEEP, SEQ), BF16),
            pltpu.VMEM((WROWS, DEEP), BF16),
            pltpu.VMEM((ROWS, SEQ), F32),
            pltpu.VMEM((TILES, DUOS, QP, TILE), F32),
            pltpu.VMEM((PAIRS, SEQ), BF16),
            pltpu.VMEM((PAIRS, SEQ), F32),
            pltpu.VMEM((TILES, 8, TILE), F32),
            pltpu.SMEM((2, TILES), jnp.int32),
        ],
        compiler_params=PARAMS,
        cost_estimate=pl.CostEstimate(
            flops=20_000_000_000, bytes_accessed=10_000_000, transcendentals=0
        ),
        name="recv_half",
    )(received, states, codes, own, fields, weights)


def own_grad_kernel(
    keys_ref, bounds, place, far, resid, field_part, g0, g1, g2, g3, grad, wide, full, hot, rows
):
    add_grad(keys_ref, bounds, resid, hot, grad, far)
    for n in range(WIDE):
        wide[n, Q * Q // 8 * 8 : PADQ, :] = jnp.zeros((PADQ - Q * Q // 8 * 8, TILE), F32)
        for c, column in enumerate(load_grad(grad, n)):
            wide[n, pl.ds(c, Q, stride=Q), :] = column[0:Q]
        rows[:, n * TILE : (n + 1) * TILE] = wide[n].astype(BF16)
    full[...] = dot(rows[...], plain_order(place))
    outs = (g0, g1, g2, g3)
    store_quarters(full, outs)
    exact = field_part[...]
    coarse = exact.astype(BF16).astype(F32)
    rest = exact - coarse
    tail = jnp.concatenate(
        [coarse[0:16], jnp.concatenate([coarse[16:24], rest[0:8]], axis=0), rest[8:24],
         jnp.zeros((16, TILE), F32)], axis=1,
    ).astype(BF16)
    for out in outs:
        out[QUARTER:TILE, :] = tail


def own_grad(keys, bounds, place, far, resid, field_part):
    return pl.pallas_call(
        own_grad_kernel,
        out_shape=(jax.ShapeDtypeStruct((TILE, PAIRS), BF16),) * 4,
        in_specs=[VMEM, SMEM] + [VMEM] * 4,
        out_specs=(VMEM,) * 4,
        scratch_shapes=[
            pltpu.VMEM((TILES, DUOS, QP, TILE), F32),
            pltpu.VMEM((WIDE, PADQ, TILE), F32),
            pltpu.VMEM((PADQ, PAIRS), F32),
            pltpu.VMEM((TILES, DEEP, SEQ), BF16),
            pltpu.VMEM((PADQ, PAIRS), BF16),
        ],
        compiler_params=PARAMS,
        cost_estimate=pl.CostEstimate(
            flops=6_000_000_000, bytes_accessed=8_000_000, transcendentals=0
        ),
        name="own_grad",
    )(keys, bounds, place, far, resid, field_part)


def join_kernel(scale, mine, r1, r2, r3, remote, out, field_out):
    total = mine[...].astype(F32) + r1[...].astype(F32)
    total = total + (r2[...].astype(F32) + r3[...].astype(F32))
    summed = remote[0].astype(F32) + remote[1].astype(F32)
    summed = summed + (remote[2].astype(F32) + remote[3].astype(F32))
    flipped = jnp.transpose(summed)
    out[...] = ((total[0:QUARTER] + flipped[0:QUARTER]) * scale).astype(SENT)
    tail = total[QUARTER:TILE]
    first = tail[:, 0:TILE]
    middle = tail[:, TILE : 2 * TILE]
    last = tail[:, 2 * TILE : 3 * TILE]
    coarse = jnp.concatenate([first, middle[0:8]], axis=0)
    rest = jnp.concatenate([middle[8:16], last], axis=0)
    field_out[...] = ((coarse + rest) * scale)[0:Q, 0:RL]


def join_parts(scale, chunks, remote):
    return pl.pallas_call(
        functools.partial(join_kernel, scale),
        out_shape=(
            jax.ShapeDtypeStruct((QUARTER, PAIRS), SENT),
            jax.ShapeDtypeStruct((Q, RL), F32),
        ),
        in_specs=[VMEM] * 5,
        out_specs=(VMEM, VMEM),
        compiler_params=SMALL,
        name="join_parts",
    )(*chunks, remote)


def place_kernel(c0, c1, c2, c3, out):
    short = Q * Q - 3 * QUARTER
    for back, part in enumerate((c0, c1, c2, c3)):
        owner = lax.rem(lax.axis_index("seq") + (4 - back), 4)

        @pl.when(owner < 3)
        def _():
            out[pl.ds(pl.multiple_of(owner * QUARTER, 8), QUARTER), :] = part[...].astype(F32)

        @pl.when(owner == 3)
        def _():
            out[3 * QUARTER : Q * Q, :] = part[0:short, :].astype(F32)


def place_parts(chunks):
    return pl.pallas_call(
        place_kernel,
        out_shape=jax.ShapeDtypeStruct((Q * Q, PAIRS), F32),
        in_specs=[VMEM] * 4,
        out_specs=VMEM,
        compiler_params=SMALL,
        name="place_parts",
    )(*chunks)


def shifted(array, k):
    return lax.ppermute(array, "seq", [(i, (i + k) % 4) for i in range(4)])


def gather_seq(array):
    return [array] + [shifted(array, k) for k in (1, 2, 3)]


def scatter_seq(quarters):
    return [quarters[0]] + [shifted(quarters[k], k) for k in (1, 2, 3)]


def swap_blocks(array):
    blocks = array.reshape(BLOCKS, CAP, array.shape[1])
    moved = lax.all_to_all(blocks, "res", split_axis=0, concat_axis=0, tiled=True)
    return moved.reshape(array.shape)


def swap_quarters(array):
    blocks = array.reshape(4 * BLOCKS, CAP, TILE)
    moved = lax.all_to_all(blocks, ("seq", "res"), split_axis=0, concat_axis=0, tiled=True)
    return moved.reshape(4, PAIRS, TILE)


def per_device(
    alignment, seq_weights, fields, couplings, pair_left, pair_slot, slot_residue, pair_count
):
    scale = Q / (SEQ * 4)
    coup = couplings.T
    pack = pack_pairs(
        coup, pair_left[None, :], pair_slot[None, :], slot_residue[None, :], pair_count[None, :]
    )
    received = swap_blocks(pack)
    states, codes, far, place, keys, bounds, field = own_field(alignment, pack, coup)
    remote_grad, resid, field_part = recv_half(received, states, codes, field, fields.T, seq_weights[None, :])
    swapped = swap_quarters(remote_grad)
    local_quarters = own_grad(keys, bounds, place, far, resid, field_part)
    local_chunks = scatter_seq(local_quarters)
    joined, field_grad = join_parts(scale, local_chunks, swapped)
    coupling_grad = place_parts(gather_seq(joined))
    return coupling_grad.T, field_grad.T


def solution(mesh):
    in_specs = (
        P(None, "seq"),
        P("seq"),
        P("res", None),
        P("res", None),
        P("res"),
        P("res"),
        P("res"),
        P("res"),
    )
    out_specs = (P("res", None), P("res", None))
    return jax.shard_map(
        per_device, mesh=mesh, in_specs=in_specs, out_specs=out_specs, check_vma=False
    )
```

```python
import functools

import jax
import jax.numpy as jnp
from jax import lax
from jax.experimental import pallas as pl
from jax.experimental.pallas import tpu as pltpu
from jax.sharding import PartitionSpec as P

Q = 21
QP = 24
RL = 48
CAP = 8
SLOTS = 4
PAIRS = 512
BLOCKS = 64
SEQ = 256
RES = 3072
TILE = 128
WIDE = PAIRS // TILE
SPAN = 64
TILES = PAIRS // SPAN
DUOS = (Q + 1) // 2
ROWS = RL * QP
WINDOW = 16
WROWS = WINDOW * QP
QUARTER = 112
PADQ = 4 * QUARTER
DEEP = DUOS * TILE
F32 = jnp.float32
BF16 = jnp.bfloat16
VMEM = pl.BlockSpec(memory_space=pltpu.VMEM)
SMEM = pl.BlockSpec(memory_space=pltpu.SMEM)
PARAMS = pltpu.CompilerParams(vmem_limit_bytes=20 * 1024 * 1024)
LARGE = pltpu.CompilerParams(vmem_limit_bytes=56 * 1024 * 1024)
SMALL = pltpu.CompilerParams(vmem_limit_bytes=16 * 1024 * 1024)
SENT = BF16


def iota(shape, dim):
    return lax.broadcasted_iota(jnp.int32, shape, dim)


def dot(x, y):
    return jnp.dot(x, y, preferred_element_type=F32)


def pack_kernel(coup, left, slot, residue, count, out, wide, held, sems):
    wide[Q * Q // 8 * 8 : PADQ, :] = jnp.zeros((PADQ - Q * Q // 8 * 8, PAIRS), F32)
    wide[0 : Q * Q, :] = coup[...].astype(F32)
    lane = iota((1, PAIRS), 1)
    bucket = lax.shift_right_logical(lane, 3)
    wanted = bucket * SLOTS + slot[...]
    pick = jnp.where(iota((BLOCKS * SLOTS, PAIRS), 0) == wanted, 1.0, 0.0).astype(BF16)
    partner = dot(jnp.broadcast_to(residue[...], (8, BLOCKS * SLOTS)).astype(F32).astype(BF16), pick)
    spread = jnp.where(iota((BLOCKS, PAIRS), 0) == bucket, 1.0, 0.0).astype(BF16)
    counts = dot(jnp.broadcast_to(count[...], (8, BLOCKS)).astype(F32).astype(BF16), spread)
    live = jnp.where((lane & (CAP - 1)).astype(F32) < counts[0:1], 1.0, 0.0)
    sub = iota((16, PAIRS), 0)
    index = jnp.where(sub == 0, left[...].astype(F32), 0.0)
    index = jnp.where(sub == 1, partner[0:1], index)
    index = jnp.where(sub == 2, live, index)
    index = jnp.where(sub == 3, lax.axis_index("res").astype(F32), index)
    index = jnp.where(sub == 4, bucket.astype(F32), index)
    copies = []
    for n in range(4):
        part = jnp.concatenate([wide[n * QUARTER : (n + 1) * QUARTER, :], index], axis=0)
        held[n] = jnp.transpose(part).astype(BF16)
        lanes = slice(n * TILE, (n + 1) * TILE)
        copies.append(pltpu.make_async_copy(held.at[n], out.at[:, lanes], sems.at[n]))
        copies[n].start()
    for copy in copies:
        copy.wait()


def pack_pairs(coup, left, slot, residue, count):
    return pl.pallas_call(
        pack_kernel,
        out_shape=jax.ShapeDtypeStruct((PAIRS, 4 * TILE), BF16),
        in_specs=[VMEM] * 5,
        out_specs=pl.BlockSpec(memory_space=pl.ANY),
        scratch_shapes=[
            pltpu.VMEM((PADQ, PAIRS), F32),
            pltpu.VMEM((4, PAIRS, TILE), BF16),
            pltpu.SemaphoreType.DMA((4,)),
        ],
        compiler_params=LARGE,
        name="pack_pairs",
    )(coup, left, slot, residue, count)


def order_half(pack, flipped, own):
    mine, other, block = (112, 113, 116) if own else (113, 112, 115)
    wide = pack.astype(F32)
    key_row = jnp.where(flipped[114:115] > 0.5, flipped[mine : mine + 1], float(RL))
    key_col = jnp.where(wide[:, 114:115] > 0.5, wide[:, mine : mine + 1], float(RL))
    lane = iota((PAIRS, PAIRS), 1).astype(F32)
    sub = iota((PAIRS, PAIRS), 0).astype(F32)
    full_row = key_row * PAIRS + lane
    full_col = key_col * PAIRS + sub
    place_row = jnp.sum(jnp.where(full_col < full_row, 1.0, 0.0), axis=0, keepdims=True)
    place_col = jnp.sum(jnp.where(full_row < full_col, 1.0, 0.0), axis=1, keepdims=True)
    to_sorted = jnp.where(place_col == lane, 1.0, 0.0).astype(BF16)
    to_plain = jnp.where(place_row == sub, 1.0, 0.0).astype(BF16)
    far = wide[:, block : block + 1] * RL + wide[:, other : other + 1]
    keys = dot(jnp.broadcast_to(key_row, (8, PAIRS)).astype(BF16), to_sorted)
    return to_sorted, to_plain, place_row, far, keys


def plain_order(place):
    return jnp.where(place[0:1] == iota((PAIRS, PAIRS), 0).astype(F32), 1.0, 0.0).astype(BF16)


def find_far(far, states, to_plain, plain):
    count = 4
    for start in range(0, BLOCKS, count):
        blocks = min(count, BLOCKS - start)
        pairs = slice(start * CAP, (start + blocks) * CAP)
        base = start * RL
        depth = min(256, RES - base)
        lane = iota((blocks * CAP, depth), 1).astype(F32).astype(BF16)
        wanted = jnp.broadcast_to(far[pairs] - float(base), lane.shape).astype(BF16)
        pick = jnp.where(wanted == lane, jnp.ones_like(lane), jnp.zeros_like(lane))
        plain[pairs, :] = dot(pick, states[base : base + depth, :].astype(BF16))
    return dot(to_plain, plain[...].astype(BF16))


def fill_hot(far, j, hot):
    tile = far[pl.ds(pl.multiple_of(j * SPAN, SPAN), SPAN), :].astype(BF16)
    one, none = jnp.ones_like(tile), jnp.zeros_like(tile)
    for c in range(2 * DUOS):
        hot[j, c * SPAN : (c + 1) * SPAN, :] = jnp.where(tile == jnp.array(c, BF16), one, none)


def halves(first, second):
    low = iota(first.shape, 1) < SPAN
    return (
        jnp.where(low, first, pltpu.roll(second, SPAN, 1)),
        jnp.where(low, pltpu.roll(first, SPAN, 1), second),
    )


def store_keys(keys, keys_ref, bounds):
    for n in range(WIDE):
        part = keys[:, n * TILE : (n + 1) * TILE]
        for i, span in enumerate(halves(part, part)):
            j = 2 * n + i
            keys_ref[j] = span
            bounds[0, j], bounds[1, j] = window_range(span)


def store_blocks(block, n, blocks):
    for d in range(DUOS):
        second = block(2 * d + 1) if 2 * d + 1 < Q else jnp.zeros((QP, TILE), F32)
        blocks[2 * n, d], blocks[2 * n + 1, d] = halves(block(2 * d), second)


def load_grad(grad, n):
    columns = []
    for d in range(DUOS):
        columns.extend(halves(grad[2 * n, d], grad[2 * n + 1, d]))
    return columns[:Q]


def window_range(keys):
    low = jnp.min(keys).astype(jnp.int32)
    high = jnp.max(jnp.where(keys < RL - 0.5, keys, -1.0)).astype(jnp.int32)
    first = low - (low & 1)
    return first, jnp.where(high >= 0, (high - first) // WINDOW + 1, 0)


def window_at(keys, first, step):
    start = first + step * WINDOW
    base = jnp.minimum(start, RL - WINDOW)
    fresh = jnp.where(keys[0:1] >= start.astype(F32), keys[0:1], -1.0)
    wide = jnp.broadcast_to(fresh, (QP, TILE))
    rows = pl.ds(pl.multiple_of(base * QP, 2 * QP), WROWS)
    return rows, [wide == (base + m).astype(F32) for m in range(WINDOW)]


def add_field(keys_ref, bounds, blocks, far, hot, lhs, field):
    def tile_step(j, carry):
        keys = keys_ref[j]
        first, count = bounds[0, j], bounds[1, j]

        @pl.when(count > 0)
        def _():
            fill_hot(far, j, hot)

        def window_step(step, carry):
            window, masks = window_at(keys, first, step)
            for d in range(DUOS):
                block = blocks[j, d]
                rows = [jnp.where(mask, block, 0.0) for mask in masks]
                lhs[:, d * TILE : (d + 1) * TILE] = jnp.concatenate(rows, axis=0).astype(BF16)
            field[window, :] += dot(lhs[...], hot[j])
            return carry

        return lax.fori_loop(0, count, window_step, carry)

    lax.fori_loop(0, TILES, tile_step, 0)


def add_grad(keys_ref, bounds, resid, hot, grad, far=None):
    grad[...] = jnp.zeros_like(grad)

    def tile_step(j, carry):
        keys = keys_ref[j]
        first, count = bounds[0, j], bounds[1, j]
        if far is not None:

            @pl.when(count > 0)
            def _():
                fill_hot(far, j, hot)

        def window_step(step, carry):
            window, masks = window_at(keys, first, step)
            rows = resid[window, :]
            for d in range(0, DUOS, 2):
                duos = min(2, DUOS - d)
                part = hot[j, d * TILE : (d + duos) * TILE, :]
                out = lax.dot_general(
                    rows, part, (((1,), (1,)), ((), ())), preferred_element_type=F32
                )
                for i in range(duos):
                    total = grad[j, d + i]
                    for m in range(WINDOW):
                        piece = out[m * QP : (m + 1) * QP, i * TILE : (i + 1) * TILE]
                        total = jnp.where(masks[m], piece, total)
                    grad[j, d + i] = total
            return carry

        return lax.fori_loop(0, count, window_step, carry)

    lax.fori_loop(0, TILES, tile_step, 0)


def store_quarters(full, outs):
    seq_index = lax.axis_index("seq")
    for k, out in enumerate(outs):
        owner = lax.rem(seq_index + k, 4)
        out[0:QUARTER, :] = full[pl.ds(pl.multiple_of(owner * QUARTER, 8), QUARTER), :].astype(BF16)


def own_field_kernel(
    alignment, pack, coup, states_out, codes_out, far_out, place_out, keys_ref, bounds, field,
    sorted_blocks, blocks, hot, lhs, codes, plain, states,
):
    chunk = 512
    parts = [slice(n * chunk, (n + 1) * chunk) for n in range(RES // chunk)]
    packed = pack[:, 0:TILE]
    flipped = jnp.transpose(packed.astype(F32))
    to_sorted, to_plain, place, far, keys = order_half(packed, flipped, True)
    place_out[...] = jnp.broadcast_to(place, (8, PAIRS))
    store_keys(keys, keys_ref, bounds)
    sorted_blocks[...] = jnp.zeros_like(sorted_blocks)
    ordered = dot(coup[...], to_sorted)
    for n in range(WIDE):
        sorted_blocks[n, 0 : Q * Q, :] = ordered[:, n * TILE : (n + 1) * TILE]
        store_blocks(lambda c: sorted_blocks[n, pl.ds(c, QP, stride=Q), :], n, blocks)
    field[...] = jnp.zeros_like(field)
    for rows in parts:
        part = alignment[rows, :]
        states[rows, :] = part.astype(F32).astype(BF16)
        states_out[rows, :] = part.astype(jnp.int8)
    mine = pl.ds(pl.multiple_of(lax.axis_index("res") * RL, 16), RL)
    codes_out[...] = states[mine, :]
    far_states = find_far(far, states, to_plain, plain)
    far_out[...] = far_states.astype(jnp.int8)
    codes[...] = far_states.astype(BF16)
    add_field(keys_ref, bounds, blocks, codes, hot, lhs, field)


def own_field(alignment, pack, coup):
    return pl.pallas_call(
        own_field_kernel,
        out_shape=(
            jax.ShapeDtypeStruct((RES, SEQ), jnp.int8),
            jax.ShapeDtypeStruct((RL, SEQ), BF16),
            jax.ShapeDtypeStruct((PAIRS, SEQ), jnp.int8),
            jax.ShapeDtypeStruct((8, PAIRS), F32),
            jax.ShapeDtypeStruct((TILES, 8, TILE), F32),
            jax.ShapeDtypeStruct((2, TILES), jnp.int32),
            jax.ShapeDtypeStruct((ROWS, SEQ), F32),
        ),
        in_specs=[VMEM, VMEM, VMEM],
        out_specs=(VMEM,) * 5 + (SMEM, VMEM),
        scratch_shapes=[
            pltpu.VMEM((WIDE, 512, TILE), F32),
            pltpu.VMEM((TILES, DUOS, QP, TILE), F32),
            pltpu.VMEM((TILES, DEEP, SEQ), BF16),
            pltpu.VMEM((WROWS, DEEP), BF16),
            pltpu.VMEM((PAIRS, SEQ), BF16),
            pltpu.VMEM((PAIRS, SEQ), F32),
            pltpu.VMEM((RES, SEQ), BF16),
        ],
        compiler_params=PARAMS,
        cost_estimate=pl.CostEstimate(
            flops=10_000_000_000, bytes_accessed=10_000_000, transcendentals=0
        ),
        name="own_field",
    )(alignment, pack, coup)


def recv_kernel(
    parts, states, codes, own, fields, weights,
    grad_out, resid_out, field_out,
    wide, sorted_blocks, blocks, hot, lhs, field, grad, far, plain, keys_ref, bounds,
):
    packed = parts[:, 0:TILE]
    flipped = jnp.transpose(packed.astype(F32))
    to_sorted, to_plain, place, far_col, keys = order_half(packed, flipped, False)
    store_keys(keys, keys_ref, bounds)
    far[...] = find_far(far_col, states, to_plain, plain).astype(BF16)
    for n in range(4):
        if n > 0:
            flipped = jnp.transpose(parts[:, n * TILE : (n + 1) * TILE].astype(F32))
        wide[n * QUARTER : (n + 1) * QUARTER, :] = flipped[0:QUARTER]
    sorted_blocks[PADQ:512, :] = jnp.zeros((512 - PADQ, PAIRS), F32)
    sorted_blocks[0:PADQ, :] = dot(wide[0:PADQ, :].astype(BF16), to_sorted)
    for n in range(WIDE):
        lanes = slice(n * TILE, (n + 1) * TILE)
        store_blocks(lambda a: sorted_blocks[a * Q : a * Q + QP, lanes], n, blocks)
    field[...] = own[...]
    add_field(keys_ref, bounds, blocks, far, hot, lhs, field)

    my_codes = codes[...].astype(F32)
    state = iota((QP, SEQ), 0).astype(F32)
    weight = weights[...]
    lane = iota((QP, TILE), 1)
    local = jnp.concatenate([fields[...], jnp.full((QP - Q, RL), -1e30, F32)], axis=0)
    field_part = jnp.zeros((QP, TILE), F32)
    ones = jnp.ones((SEQ, TILE), BF16)
    for r in range(0, RL, 2):
        pieces = []
        for m in (r, r + 1):
            logits = field[m * QP : (m + 1) * QP, :] + local[:, m : m + 1]
            top = jnp.max(logits, axis=0, keepdims=True)
            raised = jnp.exp(logits - top)
            share = weight / jnp.sum(raised, axis=0, keepdims=True)
            hot_own = jnp.where(state == my_codes[m : m + 1], weight, 0.0)
            pieces.append(raised * share - hot_own)
        resid_out[r * QP : (r + 2) * QP, :] = jnp.concatenate(pieces, axis=0).astype(BF16)
    sums = dot(resid_out[...], ones)
    for r in range(RL):
        field_part = jnp.where(lane == r, sums[r * QP : (r + 1) * QP], field_part)
    field_out[...] = field_part

    add_grad(keys_ref, bounds, resid_out, hot, grad)
    for n in range(4):
        wide[n * TILE + QUARTER : (n + 1) * TILE, :] = jnp.zeros((TILE - QUARTER, PAIRS), F32)
    last = 3 * TILE + Q * Q - 3 * QUARTER
    wide[last // 8 * 8 : 3 * TILE + QUARTER, :] = jnp.zeros((3 * TILE + QUARTER - last // 8 * 8, PAIRS), F32)
    for n in range(WIDE):
        lanes = slice(n * TILE, (n + 1) * TILE)
        for a, column in enumerate(load_grad(grad, n)):
            done = 0
            while done < Q:
                quarter, row = divmod(a * Q + done, QUARTER)
                size = min(Q - done, QUARTER - row)
                start = quarter * TILE + row
                wide[start : start + size, lanes] = column[done : done + size]
                done += size
    result = lax.dot_general(
        to_sorted, wide[...].astype(BF16), (((1,), (1,)), ((), ())), preferred_element_type=F32
    )
    for n in range(4):
        grad_out[n] = result[:, n * TILE : (n + 1) * TILE].astype(BF16)


def recv_half(received, states, codes, own, fields, weights):
    return pl.pallas_call(
        recv_kernel,
        out_shape=(
            jax.ShapeDtypeStruct((4, PAIRS, TILE), BF16),
            jax.ShapeDtypeStruct((ROWS, SEQ), BF16),
            jax.ShapeDtypeStruct((QP, TILE), F32),
        ),
        in_specs=[VMEM] * 6,
        out_specs=(VMEM,) * 3,
        scratch_shapes=[
            pltpu.VMEM((4 * TILE, PAIRS), F32),
            pltpu.VMEM((512, PAIRS), F32),
            pltpu.VMEM((TILES, DUOS, QP, TILE), F32),
            pltpu.VMEM((TILES, DEEP, SEQ), BF16),
            pltpu.VMEM((WROWS, DEEP), BF16),
            pltpu.VMEM((ROWS, SEQ), F32),
            pltpu.VMEM((TILES, DUOS, QP, TILE), F32),
            pltpu.VMEM((PAIRS, SEQ), BF16),
            pltpu.VMEM((PAIRS, SEQ), F32),
            pltpu.VMEM((TILES, 8, TILE), F32),
            pltpu.SMEM((2, TILES), jnp.int32),
        ],
        compiler_params=PARAMS,
        cost_estimate=pl.CostEstimate(
            flops=20_000_000_000, bytes_accessed=10_000_000, transcendentals=0
        ),
        name="recv_half",
    )(received, states, codes, own, fields, weights)


def own_grad_kernel(
    keys_ref, bounds, place, far, resid, field_part, g0, g1, g2, g3, grad, wide, full, hot, rows
):
    add_grad(keys_ref, bounds, resid, hot, grad, far)
    for n in range(WIDE):
        wide[n, Q * Q // 8 * 8 : PADQ, :] = jnp.zeros((PADQ - Q * Q // 8 * 8, TILE), F32)
        for c, column in enumerate(load_grad(grad, n)):
            wide[n, pl.ds(c, Q, stride=Q), :] = column[0:Q]
        rows[:, n * TILE : (n + 1) * TILE] = wide[n].astype(BF16)
    full[...] = dot(rows[...], plain_order(place))
    outs = (g0, g1, g2, g3)
    store_quarters(full, outs)
    exact = field_part[...]
    coarse = exact.astype(BF16).astype(F32)
    rest = exact - coarse
    tail = jnp.concatenate(
        [coarse[0:16], jnp.concatenate([coarse[16:24], rest[0:8]], axis=0), rest[8:24],
         jnp.zeros((16, TILE), F32)], axis=1,
    ).astype(BF16)
    for out in outs:
        out[QUARTER:TILE, :] = tail


def own_grad(keys, bounds, place, far, resid, field_part):
    return pl.pallas_call(
        own_grad_kernel,
        out_shape=(jax.ShapeDtypeStruct((TILE, PAIRS), BF16),) * 4,
        in_specs=[VMEM, SMEM] + [VMEM] * 4,
        out_specs=(VMEM,) * 4,
        scratch_shapes=[
            pltpu.VMEM((TILES, DUOS, QP, TILE), F32),
            pltpu.VMEM((WIDE, PADQ, TILE), F32),
            pltpu.VMEM((PADQ, PAIRS), F32),
            pltpu.VMEM((TILES, DEEP, SEQ), BF16),
            pltpu.VMEM((PADQ, PAIRS), BF16),
        ],
        compiler_params=PARAMS,
        cost_estimate=pl.CostEstimate(
            flops=6_000_000_000, bytes_accessed=8_000_000, transcendentals=0
        ),
        name="own_grad",
    )(keys, bounds, place, far, resid, field_part)


def join_kernel(scale, mine, r1, r2, r3, remote, out, field_out):
    total = mine[...].astype(F32) + r1[...].astype(F32)
    total = total + (r2[...].astype(F32) + r3[...].astype(F32))
    summed = remote[0].astype(F32) + remote[1].astype(F32)
    summed = summed + (remote[2].astype(F32) + remote[3].astype(F32))
    flipped = jnp.transpose(summed)
    out[...] = ((total[0:QUARTER] + flipped[0:QUARTER]) * scale).astype(SENT)
    tail = total[QUARTER:TILE]
    first = tail[:, 0:TILE]
    middle = tail[:, TILE : 2 * TILE]
    last = tail[:, 2 * TILE : 3 * TILE]
    coarse = jnp.concatenate([first, middle[0:8]], axis=0)
    rest = jnp.concatenate([middle[8:16], last], axis=0)
    field_out[...] = ((coarse + rest) * scale)[0:Q, 0:RL]


def join_parts(scale, chunks, remote):
    return pl.pallas_call(
        functools.partial(join_kernel, scale),
        out_shape=(
            jax.ShapeDtypeStruct((QUARTER, PAIRS), SENT),
            jax.ShapeDtypeStruct((Q, RL), F32),
        ),
        in_specs=[VMEM] * 5,
        out_specs=(VMEM, VMEM),
        compiler_params=SMALL,
        name="join_parts",
    )(*chunks, remote)


def place_kernel(c0, c1, c2, c3, out):
    short = Q * Q - 3 * QUARTER
    for back, part in enumerate((c0, c1, c2, c3)):
        owner = lax.rem(lax.axis_index("seq") + (4 - back), 4)

        @pl.when(owner < 3)
        def _():
            out[pl.ds(pl.multiple_of(owner * QUARTER, 8), QUARTER), :] = part[...].astype(F32)

        @pl.when(owner == 3)
        def _():
            out[3 * QUARTER : Q * Q, :] = part[0:short, :].astype(F32)


def place_parts(chunks):
    return pl.pallas_call(
        place_kernel,
        out_shape=jax.ShapeDtypeStruct((Q * Q, PAIRS), F32),
        in_specs=[VMEM] * 4,
        out_specs=VMEM,
        compiler_params=SMALL,
        name="place_parts",
    )(*chunks)


def shifted(array, k):
    return lax.ppermute(array, "seq", [(i, (i + k) % 4) for i in range(4)])


def gather_seq(array):
    return [array] + [shifted(array, k) for k in (1, 2, 3)]


def scatter_seq(quarters):
    return [quarters[0]] + [shifted(quarters[k], k) for k in (1, 2, 3)]


def swap_blocks(array):
    blocks = array.reshape(BLOCKS, CAP, array.shape[1])
    moved = lax.all_to_all(blocks, "res", split_axis=0, concat_axis=0, tiled=True)
    return moved.reshape(array.shape)


def swap_quarters(array):
    blocks = array.reshape(4 * BLOCKS, CAP, TILE)
    moved = lax.all_to_all(blocks, ("seq", "res"), split_axis=0, concat_axis=0, tiled=True)
    return moved.reshape(4, PAIRS, TILE)


def per_device(
    alignment, seq_weights, fields, couplings, pair_left, pair_slot, slot_residue, pair_count
):
    scale = Q / (SEQ * 4)
    coup = couplings.T
    pack = pack_pairs(
        coup, pair_left[None, :], pair_slot[None, :], slot_residue[None, :], pair_count[None, :]
    )
    received = swap_blocks(pack)
    states, codes, far, place, keys, bounds, field = own_field(alignment, pack, coup)
    remote_grad, resid, field_part = recv_half(received, states, codes, field, fields.T, seq_weights[None, :])
    swapped = swap_quarters(remote_grad)
    local_quarters = own_grad(keys, bounds, place, far, resid, field_part)
    local_chunks = scatter_seq(local_quarters)
    joined, field_grad = join_parts(scale, local_chunks, swapped)
    coupling_grad = place_parts(gather_seq(joined))
    return coupling_grad.T, field_grad.T


def solution(mesh):
    in_specs = (
        P(None, "seq"),
        P("seq"),
        P("res", None),
        P("res", None),
        P("res"),
        P("res"),
        P("res"),
        P("res"),
    )
    out_specs = (P("res", None), P("res", None))
    return jax.shard_map(
        per_device, mesh=mesh, in_specs=in_specs, out_specs=out_specs, check_vma=False
    )
```
